256 devices in a mesh: role: 2 (over x_hi), grp: 8 (over z), blk: 16 (over y, x_lo, core).
Axes of the slice: x: 4 (x_hi: 2, x_lo: 2; x = x_hi * 2 + x_lo), y: 4, z: 8, core: 2. Of those that a mesh axis runs over, the one named last changes fastest.
Arguments:
- prompt_hidden: bfloat16 [16384, 8192], P(('grp', 'blk'), 'role'), parts along dimension 0, may hold values from -6 to 6
- prompt_qkv: bfloat16 [16384, 5120], P(('grp', 'blk')), parts along dimension 0, may hold values from -6 to 6
- block_tenant: int32 [128], P(('grp', 'blk')), parts along dimension 0, may hold values from 0 to 1
- row_hidden: bfloat16 [32, 8192], P('grp'), parts along dimension 0, may hold values from -6 to 6
- row_qkv: bfloat16 [32, 5120], P('grp'), parts along dimension 0, may hold values from -6 to 6
- row_tenant: int32 [32], P('grp'), parts along dimension 0, may hold values from 0 to 1, as said below
- row_cache: bfloat16 [24, 2048, 1024], P('grp', 'blk'), parts along dimension 0, may hold values from -6 to 6
- row_lengths: int32 [24], P('grp'), parts along dimension 0, may hold values from 1 to 2048, as said below
- qkv_down: bfloat16 [2, 8192, 192], P(None, ('role', 'blk')), may hold values from -0.0625 to 0.0625
- qkv_up: bfloat16 [2, 64, 5120], P(None, None, 'blk'), may hold values from -0.75 to 0.75
- out_down: bfloat16 [2, 4096, 64], P(None, 'blk'), may hold values from -0.09375 to 0.09375
- out_up: bfloat16 [2, 64, 8192], P(None, None, ('role', 'blk')), may hold values from -0.75 to 0.75
Outputs:
- prompt_out: bfloat16 [16384, 8192], P(('grp', 'blk'), 'role'), parts along dimension 0
- row_out: bfloat16 [32, 8192], P('grp', ('role', 'blk')), parts along dimension 0
The draws below stay inside these ranges and needn't reach their ends.
There are 8 independent parts, one for each index of `grp`. The reference program is written for one: setup_inputs(seed, part) draws one part's arguments, and reference() takes and returns one part's arrays. A program takes and returns all parts, laid end to end along the dimension named above; an argument that names none is the same for every part. Nothing has to cross between parts.
Inputs may be any that keep to these rules, and one draw needn't show every extreme that they name: `row_lengths`: one of the rows has exactly 2048 valid positions. `row_tenant`: the rows name at least two different adapters.
All inputs are finite; a program needn't handle non-finite values.
Results may differ from the reference program's by a relative error of at most 0.03.
Values may be sent and summed in bfloat16 or wider, within the bound.
No kernel may reach another device: no remote copies, remote signals or barrier semaphores. Data moves between devices by JAX's collectives and lax.ppermute only.
A program may use at most 64 MiB of HBM per device.

```python
import jax
import jax.numpy as jnp
from jax import lax

D = 8192
QUERY_HEADS = 32
KEY_VALUE_HEADS = 4
HEAD_SIZE = 128
RANK = 64
ADAPTERS = 2
BLOCK = 128
DECODE_ROWS = 4
PROMPT_LENGTH = 2048
NBLOCKS = 16
WQKV = 5120


inserted_count = 4


def sign_pattern(key, count):
    return jnp.where(jax.random.bernoulli(key, 0.5, (count, HEAD_SIZE)), 1.0, -1.0).astype(jnp.float32)


def prompt_layout(key):
    key = jax.random.fold_in(key, 101)
    key_pos, shared_key_head = jax.random.split(key)
    segment_size = PROMPT_LENGTH // inserted_count
    quarter = segment_size // 4
    offsets = jax.random.randint(key_pos, (inserted_count, 3), 0, quarter)
    starts = jnp.arange(inserted_count, dtype=jnp.int32) * segment_size
    head_number = jax.random.randint(shared_key_head, (inserted_count,), 0, KEY_VALUE_HEADS)
    return (starts + offsets[:, 0], starts + quarter + offsets[:, 1], starts + 2 * quarter + offsets[:, 2], head_number)


def plant_prompt(base_values, layout, sign_rows, key_level, strengths):
    first_key, second_key, query_row, head_number = layout
    group_width = QUERY_HEADS // KEY_VALUE_HEADS
    positions = jnp.arange(PROMPT_LENGTH, dtype=jnp.int32)[:, None]
    column_list = jnp.arange(WQKV, dtype=jnp.int32)[None, :]
    root_size = jnp.sqrt(jnp.float32(HEAD_SIZE))
    result = base_values
    for plant_id in range(inserted_count):
        pattern = jnp.take(sign_rows[plant_id], column_list % HEAD_SIZE)
        key_start = QUERY_HEADS * HEAD_SIZE + head_number[plant_id] * HEAD_SIZE
        in_key = (column_list >= key_start) & (column_list < key_start + HEAD_SIZE)
        query_start = head_number[plant_id] * group_width * HEAD_SIZE
        in_query = (column_list >= query_start) & (column_list < query_start + group_width * HEAD_SIZE)
        shrink = 1.0 - 2.0 / (strengths[plant_id] * key_level * root_size)
        result = jnp.where((positions == first_key[plant_id]) & in_key, key_level * pattern, result)
        result = jnp.where((positions == second_key[plant_id]) & in_key, key_level * shrink * pattern, result)
        result = jnp.where((positions == query_row[plant_id]) & in_query, strengths[plant_id] * pattern, result)
    return result


def draw_prompt_hidden(key, part):
    first_key, second_key, query_row, head_number = prompt_layout(key)
    key = jax.random.fold_in(key, 13)
    base_values = jnp.clip(jax.random.normal(key, (PROMPT_LENGTH, D), jnp.float32), -6.0, 6.0)
    positions = jnp.arange(PROMPT_LENGTH, dtype=jnp.int32)[:, None]
    quiet_rows = jnp.any((positions == first_key[None, :]) | (positions == second_key[None, :]), axis=1)
    return (base_values * jnp.where(quiet_rows, 0.05, 1.0)[:, None]).astype(jnp.bfloat16)


def draw_prompt_qkv(key, part):
    layout = prompt_layout(key)
    key = jax.random.fold_in(key, 11)
    key_base, key_sign, key_level = jax.random.split(key, 3)
    sign_rows = sign_pattern(key_sign, inserted_count)
    fractions = jax.random.uniform(key_level, (inserted_count,), jnp.float32)
    base_values = jnp.clip(jax.random.normal(key_base, (PROMPT_LENGTH, WQKV), jnp.float32), -6.0, 6.0)
    result = plant_prompt(base_values, layout, sign_rows, 5.0, 2.0 + 2.0 * fractions)
    return result.astype(jnp.bfloat16)


def draw_row_tenant(key, part):
    key = jax.random.fold_in(key, 23)
    values = jax.random.randint(key, (DECODE_ROWS,), 0, ADAPTERS)
    first_value = (values[1] + 1) % ADAPTERS
    return jnp.where(jnp.arange(DECODE_ROWS) == 0, first_value, values).astype(jnp.int32)


def cache_lengths(key):
    key = jax.random.fold_in(key, 201)
    key_values, key_choice = jax.random.split(key)
    values = jax.random.randint(key_values, (DECODE_ROWS - 1,), 1, PROMPT_LENGTH + 1)
    chosen = jax.random.randint(key_choice, (), 0, DECODE_ROWS - 1)
    return jnp.where(jnp.arange(DECODE_ROWS - 1) == chosen, PROMPT_LENGTH, values).astype(jnp.int32)


def cache_layout(key):
    lengths = cache_lengths(key)
    key = jax.random.fold_in(key, 202)
    key_pos, shared_key_head, key_sign, key_frac = jax.random.split(key, 4)
    picked_values = jax.random.randint(key_pos, (DECODE_ROWS - 1, 2), 0, PROMPT_LENGTH)
    first_key = picked_values[:, 0] % lengths
    second_key = (first_key + 1 + picked_values[:, 1] % jnp.maximum(lengths - 1, 1)) % lengths
    head_number = jax.random.randint(shared_key_head, (DECODE_ROWS - 1,), 0, KEY_VALUE_HEADS)
    sign_rows = sign_pattern(key_sign, DECODE_ROWS - 1)
    fractions = jax.random.uniform(key_frac, (DECODE_ROWS - 1,), jnp.float32)
    return (first_key, second_key, head_number, sign_rows, fractions)


def plant_cache(base_values, first_key, second_key, head_number, sign_rows, key_level, strengths):
    positions = jnp.arange(PROMPT_LENGTH, dtype=jnp.int32)[None, :, None]
    flattened_columns = jnp.arange(2 * KEY_VALUE_HEADS * HEAD_SIZE, dtype=jnp.int32)
    column_list = flattened_columns[None, None, :]
    pattern = sign_rows[:, flattened_columns % HEAD_SIZE][:, None, :]
    head_start = (head_number * HEAD_SIZE)[:, None, None]
    in_key = (column_list >= head_start) & (column_list < head_start + HEAD_SIZE)
    root_size = jnp.sqrt(jnp.float32(HEAD_SIZE))
    shrink = (1.0 - 2.0 / (strengths * key_level * root_size))[:, None, None]
    result = jnp.where((positions == first_key[:, None, None]) & in_key, key_level * pattern, base_values)
    result = jnp.where((positions == second_key[:, None, None]) & in_key, key_level * shrink * pattern, result)
    return result


def plant_queries(base_values, head_number, sign_rows, strengths):
    group_width = QUERY_HEADS // KEY_VALUE_HEADS
    column_list = jnp.arange(WQKV, dtype=jnp.int32)
    pattern = sign_rows[:, column_list % HEAD_SIZE]
    query_start = (head_number * group_width * HEAD_SIZE)[:, None]
    in_query = (column_list[None, :] >= query_start) & (column_list[None, :] < query_start + group_width * HEAD_SIZE)
    planted = jnp.where(in_query, strengths[:, None] * pattern, base_values[1:])
    return jnp.concatenate([base_values[:1], planted], axis=0)


def draw_row_lengths(key, part):
    lengths = cache_lengths(key)
    return lengths


def draw_row_cache(key, part):
    first_key, second_key, head_number, sign_rows, fractions = cache_layout(key)
    key = jax.random.fold_in(key, 17)
    tensor_shape = (DECODE_ROWS - 1, PROMPT_LENGTH, 2 * KEY_VALUE_HEADS * HEAD_SIZE)
    base_values = jnp.clip(jax.random.normal(key, tensor_shape, jnp.float32), -6.0, 6.0)
    result = plant_cache(base_values, first_key, second_key, head_number, sign_rows, 5.0, 2.0 + 2.0 * fractions)
    return result.astype(jnp.bfloat16)


def draw_row_qkv(key, part):
    first_key, second_key, head_number, sign_rows, fractions = cache_layout(key)
    key = jax.random.fold_in(key, 19)
    tensor_shape = (DECODE_ROWS, WQKV)
    base_values = jnp.clip(jax.random.normal(key, tensor_shape, jnp.float32), -6.0, 6.0)
    result = plant_queries(base_values, head_number, sign_rows, 2.0 + 2.0 * fractions)
    return result.astype(jnp.bfloat16)


def touch_ends(drawn, key, smallest, high):
    longest = drawn.shape.index(max(drawn.shape))
    spots = []
    for shift in (0, 1):
        where = [jax.random.randint(jax.random.fold_in(key, axis), (), 0, length) for axis, length in enumerate(drawn.shape)]
        where[longest] = (where[longest] + shift) % drawn.shape[longest]
        spots.append(tuple(where))
    return drawn.at[spots[0]].set(smallest).at[spots[1]].set(high)


def block_scale(key, dims, cuts, smallest, high):
    def one(position, parts):
        steps = jax.random.uniform(jax.random.fold_in(jax.random.fold_in(key, 6), position), (parts,), jnp.float32, smallest / len(cuts), high / len(cuts))
        return jnp.repeat(jnp.exp(steps), dims[position] // parts).reshape((-1,) + (1,) * (len(dims) - position - 1))

    level = one(*cuts[0])
    for cut in cuts[1:]:
        level = level * one(*cut)
    return level


def centred(stream_key, extent, deviation, limit, pieces=(), kind=jnp.bfloat16):
    entries = jax.random.normal(stream_key, extent, jnp.float32) * deviation
    if len(pieces) > 0:
        entries = block_scale(stream_key, extent, pieces, -0.22, 0.18) * entries
    return jnp.clip(entries, min=-limit, max=limit).astype(kind)


def setup_inputs(seed: int = 0, part: int = 0) -> dict:
    streams_of = jax.random.split(jax.random.key(seed), 13)
    own_keys = jax.random.split(jax.random.fold_in(streams_of[12], part), 13)
    return {
        "prompt_hidden": draw_prompt_hidden(jax.random.fold_in(jax.random.fold_in(streams_of[12], part), 71), part),
        "prompt_qkv": draw_prompt_qkv(jax.random.fold_in(jax.random.fold_in(streams_of[12], part), 71), part),
        "block_tenant": touch_ends(jax.random.randint(own_keys[2], (NBLOCKS,), 0, ADAPTERS), jax.random.fold_in(own_keys[2], 1), 0, ADAPTERS - 1).astype(jnp.int32),
        "row_hidden": centred(own_keys[3], (DECODE_ROWS, D), 1.0, 6.0),
        "row_qkv": draw_row_qkv(jax.random.fold_in(jax.random.fold_in(streams_of[12], part), 71), part),
        "row_tenant": draw_row_tenant(jax.random.fold_in(jax.random.fold_in(streams_of[12], part), 71), part),
        "row_cache": draw_row_cache(jax.random.fold_in(jax.random.fold_in(streams_of[12], part), 71), part),
        "row_lengths": draw_row_lengths(jax.random.fold_in(jax.random.fold_in(streams_of[12], part), 71), part),
        "qkv_down": centred(streams_of[8], (ADAPTERS, D, 3 * RANK), D ** -0.5, 0.0625, ((1, 32),)),
        "qkv_up": centred(streams_of[9], (ADAPTERS, RANK, WQKV), RANK ** -0.5, 0.75, ((2, 16),)),
        "out_down": centred(streams_of[10], (ADAPTERS, QUERY_HEADS * HEAD_SIZE, RANK), (QUERY_HEADS * HEAD_SIZE) ** -0.5, 0.09375, ((1, 16),)),
        "out_up": centred(streams_of[11], (ADAPTERS, RANK, D), RANK ** -0.5, 0.75, ((2, 32),)),
    }


NEGATIVE_FILLER = -1e30


def add_low_rank(base_rows, low_rank, up_matrix):
    column_list = jnp.arange(base_rows.shape[1], dtype=jnp.int32)
    column_group = (column_list >= QUERY_HEADS * HEAD_SIZE).astype(jnp.int32) + (column_list >= (QUERY_HEADS + KEY_VALUE_HEADS) * HEAD_SIZE).astype(jnp.int32)
    total_sum = base_rows.astype(jnp.float32)
    for group_id in range(3):
        product = jnp.dot(low_rank[:, group_id * RANK:(group_id + 1) * RANK], up_matrix, preferred_element_type=jnp.float32)
        total_sum = total_sum + jnp.where(column_group[None, :] == group_id, product, jnp.float32(0.0))
    return total_sum.astype(jnp.bfloat16)


def rounded_float(values):
    return lax.optimization_barrier(values.astype(jnp.bfloat16)).astype(jnp.float32)


def prompt_projection(prompt_hidden, prompt_qkv, block_tenant, qkv_down, qkv_up):
    hidden_blocks = prompt_hidden.reshape(NBLOCKS, BLOCK, D)
    base_blocks = prompt_qkv.reshape(NBLOCKS, BLOCK, WQKV)

    def one_block(inputs):
        hidden_rows, base_rows, tenant = inputs
        low_rank = jnp.dot(hidden_rows, qkv_down[tenant], preferred_element_type=jnp.float32).astype(jnp.bfloat16)
        return add_low_rank(base_rows, low_rank, qkv_up[tenant])

    return lax.map(one_block, (hidden_blocks, base_blocks, block_tenant.astype(jnp.int32))).reshape(PROMPT_LENGTH, WQKV)


def prompt_attention(prompt_projected):
    group_width = QUERY_HEADS // KEY_VALUE_HEADS
    score_scale = HEAD_SIZE ** -0.5
    query_matrix = prompt_projected[:, :QUERY_HEADS * HEAD_SIZE].reshape(PROMPT_LENGTH, KEY_VALUE_HEADS, group_width, HEAD_SIZE).astype(jnp.float32)
    key_matrix_rows = prompt_projected[:, QUERY_HEADS * HEAD_SIZE:(QUERY_HEADS + KEY_VALUE_HEADS) * HEAD_SIZE].reshape(PROMPT_LENGTH, KEY_VALUE_HEADS, HEAD_SIZE).astype(jnp.float32)
    value_matrix_rows = prompt_projected[:, (QUERY_HEADS + KEY_VALUE_HEADS) * HEAD_SIZE:].reshape(PROMPT_LENGTH, KEY_VALUE_HEADS, HEAD_SIZE).astype(jnp.float32)
    key_pos = jnp.arange(PROMPT_LENGTH, dtype=jnp.int32)

    def one_block(block_id):
        start_row = (block_id * BLOCK).astype(jnp.int32)
        query_rows = lax.dynamic_slice_in_dim(query_matrix, start_row, BLOCK, 0)
        scores = jnp.einsum("qkgd,nkd->kgqn", query_rows, key_matrix_rows) * score_scale
        query_pos = start_row + jnp.arange(BLOCK, dtype=jnp.int32)
        allowed = key_pos[None, :] <= query_pos[:, None]
        scores = jnp.where(allowed, scores, NEGATIVE_FILLER)
        row_max = jnp.max(scores, axis=-1, keepdims=True)
        weights = jnp.where(allowed, jnp.exp(scores - row_max), jnp.float32(0.0))
        weight_sum = jnp.sum(weights, axis=-1)
        numerator = jnp.einsum("kgqn,nkd->kgqd", rounded_float(weights), value_matrix_rows)
        context = numerator / weight_sum[..., None]
        return jnp.transpose(context, (2, 0, 1, 3)).reshape(BLOCK, QUERY_HEADS * HEAD_SIZE).astype(jnp.bfloat16)

    return lax.map(one_block, jnp.arange(NBLOCKS, dtype=jnp.int32)).reshape(PROMPT_LENGTH, QUERY_HEADS * HEAD_SIZE)


def row_attention(row_projected, prompt_projected, row_cache, row_lengths):
    group_width = QUERY_HEADS // KEY_VALUE_HEADS
    score_scale = HEAD_SIZE ** -0.5
    cache_entries = jnp.concatenate([prompt_projected[None, :, QUERY_HEADS * HEAD_SIZE:], row_cache], axis=0)
    limits = jnp.concatenate([jnp.full((1,), PROMPT_LENGTH, jnp.int32), row_lengths.astype(jnp.int32)])
    positions = jnp.arange(PROMPT_LENGTH, dtype=jnp.int32)
    usable = positions[None, :] < limits[:, None]
    query_matrix = row_projected[:, :QUERY_HEADS * HEAD_SIZE].reshape(DECODE_ROWS, KEY_VALUE_HEADS, group_width, HEAD_SIZE).astype(jnp.float32)
    local_keys = row_projected[:, QUERY_HEADS * HEAD_SIZE:(QUERY_HEADS + KEY_VALUE_HEADS) * HEAD_SIZE].reshape(DECODE_ROWS, KEY_VALUE_HEADS, HEAD_SIZE).astype(jnp.float32)
    local_values = row_projected[:, (QUERY_HEADS + KEY_VALUE_HEADS) * HEAD_SIZE:].reshape(DECODE_ROWS, KEY_VALUE_HEADS, HEAD_SIZE).astype(jnp.float32)
    stored_keys = cache_entries[:, :, :KEY_VALUE_HEADS * HEAD_SIZE].reshape(DECODE_ROWS, PROMPT_LENGTH, KEY_VALUE_HEADS, HEAD_SIZE).astype(jnp.float32)
    stored_values = cache_entries[:, :, KEY_VALUE_HEADS * HEAD_SIZE:].reshape(DECODE_ROWS, PROMPT_LENGTH, KEY_VALUE_HEADS, HEAD_SIZE).astype(jnp.float32)
    scores = jnp.einsum("rkgd,rnkd->rkgn", query_matrix, stored_keys) * score_scale
    scores = jnp.where(usable[:, None, None, :], scores, NEGATIVE_FILLER)
    own_score = jnp.einsum("rkgd,rkd->rkg", query_matrix, local_keys) * score_scale
    top_max = jnp.maximum(jnp.max(scores, axis=-1), own_score)
    weights = jnp.where(usable[:, None, None, :], jnp.exp(scores - top_max[..., None]), jnp.float32(0.0))
    own_weight = jnp.exp(own_score - top_max)
    denominator = jnp.sum(weights, axis=-1) + own_weight
    numerator = jnp.einsum("rkgn,rnkd->rkgd", rounded_float(weights), stored_values)
    numerator = numerator + jnp.einsum("rkg,rkd->rkgd", rounded_float(own_weight), local_values)
    return (numerator / denominator[..., None]).reshape(DECODE_ROWS, QUERY_HEADS * HEAD_SIZE).astype(jnp.bfloat16)


def reference(prompt_hidden, prompt_qkv, block_tenant, row_hidden, row_qkv, row_tenant, row_cache, row_lengths, qkv_down, qkv_up, out_down, out_up):
    prompt_projected = prompt_projection(prompt_hidden, prompt_qkv, block_tenant, qkv_down, qkv_up)
    prompt_context = prompt_attention(prompt_projected)

    def out_block(inputs):
        context_rows, tenant = inputs
        factor_rows = jnp.dot(context_rows, out_down[tenant], preferred_element_type=jnp.float32).astype(jnp.bfloat16)
        return jnp.dot(factor_rows, out_up[tenant], preferred_element_type=jnp.float32).astype(jnp.bfloat16)

    prompt_out = lax.map(out_block, (prompt_context.reshape(NBLOCKS, BLOCK, QUERY_HEADS * HEAD_SIZE), block_tenant.astype(jnp.int32))).reshape(PROMPT_LENGTH, D)

    def row_proj_one(inputs):
        hidden_row, base_row, tenant = inputs
        low_rank = jnp.dot(hidden_row[None, :], qkv_down[tenant], preferred_element_type=jnp.float32).astype(jnp.bfloat16)
        return add_low_rank(base_row[None, :], low_rank, qkv_up[tenant])[0]

    row_projected = lax.map(row_proj_one, (row_hidden, row_qkv, row_tenant.astype(jnp.int32)))
    row_context = row_attention(row_projected, prompt_projected, row_cache, row_lengths)

    def row_out_one(inputs):
        context_row, tenant = inputs
        factor_row = jnp.dot(context_row[None, :], out_down[tenant], preferred_element_type=jnp.float32).astype(jnp.bfloat16)
        return jnp.dot(factor_row, out_up[tenant], preferred_element_type=jnp.float32).astype(jnp.bfloat16)[0]

    row_out = lax.map(row_out_one, (row_context, row_tenant.astype(jnp.int32)))
    return prompt_out, row_out
```

```python
import jax
import jax.numpy as jnp
from jax import lax
from jax.experimental import pallas as pl
from jax.experimental.pallas import tpu as pltpu
from jax.sharding import PartitionSpec as P

HEADS = 8
HEAD = 128
RANK = 64
BLOCK = 128
CHIPS = 8
CHUNK = 256
ROWS = 16
LIVE = 4
SCALE = HEAD ** -0.5
LOG2E = 1.4426950408889634
NEG = -1e30
F32 = jnp.float32
BF16 = jnp.bfloat16
MIB = 1 << 20

ROLE, CHIP, CORE, OWN, ROW_T, LENGTH, HEAD_ID, HEAD_OTHER, SCALARS = 0, 1, 2, 3, 4, 8, 11, 12, 13


def nt(a, b):
    return lax.dot_general(a, b, (((1,), (1,)), ((), ())), preferred_element_type=F32)


def nn(a, b):
    return jnp.dot(a, b, preferred_element_type=F32)


def aligned(index, size):
    return pl.ds(pl.multiple_of(index * size, size), size)


def call(body, scalars, args, in_specs, outs, scratch=(), limit=16):
    def whole(shape):
        zeros = (0,) * len(shape)
        return pl.BlockSpec(shape, lambda i, *s: zeros)

    specs = [whole(a.shape) if spec is None else spec for a, spec in zip(args, in_specs)]
    return pl.pallas_call(
        body,
        grid_spec=pltpu.PrefetchScalarGridSpec(
            num_scalar_prefetch=len(scalars),
            grid=(1,),
            in_specs=specs,
            out_specs=[whole(o.shape) for o in outs],
            scratch_shapes=list(scratch),
        ),
        out_shape=outs,
        compiler_params=pltpu.CompilerParams(vmem_limit_bytes=limit * MIB),
    )(*scalars, *args)


def spec(shape, place):
    return pl.BlockSpec(shape, lambda i, ids, *s: place(ids))


def shape(dims, dtype=BF16):
    return jax.ShapeDtypeStruct(dims, dtype)


STEPS = ((0, 0), (0, 1), (1, 0), (3, 0), (1, 1), (3, 1), (2, 0), (2, 1))


def source(chip, step):
    dy, dx = step
    return lax.rem(chip // 2 + dy, 4) * 2 + (lax.rem(chip, 2) ^ dx)


def gather_chips(value):
    def get(value, step):
        pairs = []
        for i in range(2 * CHIPS):
            y, x, core = i // 4, i // 2 % 2, i % 2
            pairs.append(((y + step[0]) % 4 * 4 + (x ^ step[1]) * 2 + core, i))
        return lax.ppermute(value, "blk", pairs)

    up = get(value, (1, 0))
    down_across = get(value, (3, 1))
    across = get(value, (0, 1))
    down = get(value, (3, 0))
    up_across = get(value, (1, 1))
    far = get(up, (1, 0))
    far_across = get(down_across, (3, 0))
    return [value, across, up, down, up_across, down_across, far, far_across]


def pack_body(ids, up, down, out_up, out):
    def columns(main, tail, at):
        for t in range(2):
            out[t] = up[t, :, main : main + CHUNK]
            out[2, :, t * HEAD : (t + 1) * HEAD] = jnp.zeros((RANK, HEAD), BF16)
            out[2, :, t * HEAD + at : t * HEAD + at + RANK] = up[t, :, tail : tail + RANK]

    pl.when(ids[CORE] == 0)(lambda: columns(0, CHUNK, 0))
    pl.when(ids[CORE] == 1)(lambda: columns(RANK, 0, RANK))
    for t in range(2):
        out[3 + t] = down[t]
        out[5 + t] = out_up[t]


def low_body(ids, oth, hid, hid_oth, row_hid, *rest):
    weights, out = rest[:CHIPS], rest[CHIPS]
    role, chip, core = ids[ROLE], ids[CHIP], ids[CORE]
    own_t, oth_t = ids[OWN], oth[0]
    sums = [jnp.zeros((n, 3 * RANK), F32) for n in (BLOCK, BLOCK, ROWS, ROWS)]
    for w, step in zip(weights, STEPS):
        src = source(chip, step)
        x_own = hid[:, aligned(2 * src + core, CHUNK)]
        x_oth = hid_oth[:, aligned(2 * src + core, CHUNK)]
        x_row = row_hid[:, aligned(role * 2 * CHIPS + 2 * src + core, CHUNK)]
        sums[0] += nt(x_own, w[own_t])
        sums[1] += nt(x_oth, w[oth_t])
        sums[2] += nt(x_row, w[0])
        sums[3] += nt(x_row, w[1])
    out[aligned(core, BLOCK), :] = sums[0].astype(BF16)
    out[aligned(1 - core, BLOCK), :] = sums[1].astype(BF16)
    out[2 * BLOCK :, :] = jnp.where(row_mask(ids, ROWS, 3 * RANK), sums[3], sums[2]).astype(BF16)


def row_mask(ids, rows, width):
    at = lax.broadcasted_iota(jnp.int32, (rows, width), 0)
    mask = jnp.zeros((rows, width), jnp.int32)
    for r in range(LIVE):
        mask = jnp.where(at == r, ids[ROW_T + r], mask)
    return mask == 1


def split3(x):
    hi = x.astype(BF16).astype(F32)
    mid = (x - hi).astype(BF16).astype(F32)
    return hi, mid, x - hi - mid


def proj_body(
    ids, oth, mine, theirs, q, k, v, oq, ok, ov, rq, rk, rv, ck, cv, ock, ocv, up0, up1, tail, q_out, kv_out, upb
):
    chip, core, head = ids[CHIP], ids[CORE], ids[HEAD_ID]
    for src in range(CHIPS):
        for t, up in enumerate((up0, up1)):
            lanes = slice(t * HEAD, (t + 1) * HEAD)
            upb[src, t, :, : 2 * HEAD] = up[2 * src, 0]
            upb[src, t, :, 2 * HEAD : 3 * HEAD] = tail[2 * src, 0, :, lanes] + tail[2 * src + 1, 0, :, lanes]
            upb[src, t, :, 3 * HEAD :] = up[2 * src + 1, 0]
    low = (mine[...].astype(F32) + theirs[...].astype(F32)).astype(BF16)
    own_rows, oth_rows = aligned(core, BLOCK), aligned(1 - core, BLOCK)
    low_own = (mine[own_rows, :].astype(F32) + theirs[own_rows, :].astype(F32)).astype(BF16)
    low_oth = (mine[oth_rows, :].astype(F32) + theirs[oth_rows, :].astype(F32)).astype(BF16)
    low_row = low[2 * BLOCK :]
    mask = row_mask(ids, ROWS, HEAD)
    row_q = []
    new_k = new_v = k_own = k_oth = v_own = v_oth = None
    for j in range(HEADS + 2):
        group = max(j - HEADS + 1, 0)
        tile = head * HEADS + j if j < HEADS else head + (32 if j == HEADS else 36)
        src, off = lax.div(tile, 5), lax.rem(tile, 5)
        columns = aligned(off, HEAD)
        part = slice(group * RANK, (group + 1) * RANK)
        here = slice(j * HEAD, (j + 1) * HEAD)
        base = (q[:, here] if j < HEADS else (k if j == HEADS else v)[...]).astype(F32)
        row_base = (rq[:, here] if j < HEADS else (rk if j == HEADS else rv)[...]).astype(F32)
        got_own = (base + nn(low_own[:, part], upb[src, ids[OWN], :, columns])).astype(BF16)
        oth_base = (oq[:, here] if j < HEADS else (ok if j == HEADS else ov)[...]).astype(F32)
        got_oth = (oth_base + nn(low_oth[:, part], upb[src, oth[0], :, columns])).astype(BF16)
        row_terms = [nn(low_row[:, part], upb[src, t, :, columns]) for t in range(2)]
        got_row = (row_base + jnp.where(mask, row_terms[1], row_terms[0])).astype(BF16)
        if j < HEADS:
            q_out[own_rows, here] = got_own
            q_out[oth_rows, here] = got_oth
            row_q.append(got_row)
        elif j == HEADS:
            kv_out[own_rows, :HEAD] = got_own
            kv_out[oth_rows, :HEAD] = got_oth
            k_own, k_oth, new_k = got_own, got_oth, got_row
        else:
            kv_out[own_rows, HEAD:] = got_own
            kv_out[oth_rows, HEAD:] = got_oth
            v_own, v_oth, new_v = got_own, got_oth, got_row

    count = HEADS * ROWS
    queries = jnp.concatenate(row_q, axis=0)
    row_id = lax.rem(lax.broadcasted_iota(jnp.int32, (count, BLOCK), 0), ROWS)
    lane = lax.broadcasted_iota(jnp.int32, (count, BLOCK), 1)
    halves = []
    for at, first in ((core, 0), (1 - core, 1)):
        scores = nt(queries, k_oth if first else k_own)
        valid = jnp.full((count, BLOCK), 1, jnp.int32)
        position = (2 * chip + at) * BLOCK + lane
        for r in range(LIVE - 1):
            keys = ock[r] if first else ck[r]
            this = row_id == r + 1
            scores = jnp.where(this, nt(queries, keys), scores)
            valid = jnp.where(this, (position < ids[LENGTH + r]).astype(jnp.int32), valid)
        halves.append((jnp.where(valid == 1, scores * SCALE, NEG), valid == 1))
    own_lane = lax.broadcasted_iota(jnp.int32, (count, ROWS), 1)
    own_row = lax.rem(lax.broadcasted_iota(jnp.int32, (count, ROWS), 0), ROWS)
    first_chip = chip == 0
    own_score = jnp.where((own_lane == own_row) & first_chip, nt(queries, new_k) * SCALE, NEG)
    top = jnp.max(jnp.maximum(halves[0][0], halves[1][0]), axis=1, keepdims=True)
    top = jnp.maximum(top, jnp.max(own_score, axis=1, keepdims=True))
    own_weight = jnp.where((own_lane == own_row) & first_chip, jnp.exp(own_score - top), 0.0)
    total = jnp.sum(own_weight, axis=1, keepdims=True)
    acc = nn(own_weight.astype(BF16), new_v)
    for first, (scores, valid) in enumerate(halves):
        weights = jnp.where(valid, jnp.exp(scores - top), 0.0)
        total = total + jnp.sum(weights, axis=1, keepdims=True)
        for r in range(LIVE):
            if r == 0:
                values = v_oth if first else v_own
            else:
                values = ocv[r - 1] if first else cv[r - 1]
            acc = acc + nn(jnp.where(row_id == r, weights, 0.0).astype(BF16), values)
    stats = jnp.zeros((count, HEAD), F32)
    for place, value in enumerate(split3(top) + split3(total)):
        stats = jnp.where(lane // 16 == place, value, stats)
    keep_row = lax.broadcasted_iota(jnp.int32, (HEADS * LIVE, count), 0)
    keep_from = lax.broadcasted_iota(jnp.int32, (HEADS * LIVE, count), 1)
    keep = jnp.where((keep_row // LIVE) * ROWS + keep_row % LIVE == keep_from, 1.0, 0.0).astype(BF16)
    kv_out[2 * BLOCK :, :HEAD] = nn(keep, acc.astype(BF16)).astype(BF16)
    kv_out[2 * BLOCK :, HEAD:] = nn(keep, stats.astype(BF16)).astype(BF16)


def attend_body(ids, q, *rest):
    kvs, (ctx, row_ctx), (keys, values) = rest[:CHIPS], rest[CHIPS : CHIPS + 2], rest[CHIPS + 2 :]
    chip = ids[CHIP]
    span = 2 * BLOCK
    values[:, HEAD:] = jnp.ones((CHIPS * span, HEAD), BF16)
    for k in range(CHIPS):
        keys[aligned(source(chip, STEPS[k]), span), :] = kvs[k][:span, :HEAD]
        values[aligned(source(chip, STEPS[k]), span), :HEAD] = kvs[k][:span, HEAD:]

    def branch(chips):
        below = (chips - 1) * span

        def one_head(j, carry):
            columns = aligned(j, HEAD)
            queries = q[:, columns]
            diagonal = nt(queries, keys[below : below + span, :])
            row = lax.broadcasted_iota(jnp.int32, (span, span), 0)
            col = lax.broadcasted_iota(jnp.int32, (span, span), 1)
            diagonal = jnp.where(col <= row, diagonal, NEG)
            top = jnp.max(diagonal, axis=1, keepdims=True)
            if chips > 1:
                scores = nt(queries, keys[:below, :])
                top = jnp.maximum(top, jnp.max(scores, axis=1, keepdims=True))
            weights = jnp.exp2((diagonal - top) * (SCALE * LOG2E)).astype(BF16)
            acc = nn(weights, values[below : below + span, :])
            if chips > 1:
                weights = jnp.exp2((scores - top) * (SCALE * LOG2E)).astype(BF16)
                acc = acc + nn(weights, values[:below, :])
            ctx[:, columns] = (acc[:, :HEAD] / acc[:, HEAD:]).astype(BF16)
            return carry

        lax.fori_loop(0, HEADS, one_head, 0)

    for chips in range(1, CHIPS + 1):
        pl.when(chip == chips - 1)(lambda chips=chips: branch(chips))

    tops, totals, accs = [], [], []
    for k in range(CHIPS):
        stats = kvs[k][span:, HEAD:].astype(F32)
        tops.append(stats[:, 0:1] + stats[:, 16:17] + stats[:, 32:33])
        totals.append(stats[:, 48:49] + stats[:, 64:65] + stats[:, 80:81])
        accs.append(kvs[k][span:, :HEAD].astype(F32))
    top = tops[0]
    for value in tops[1:]:
        top = jnp.maximum(top, value)
    total, acc = 0.0, 0.0
    for k in range(CHIPS):
        factor = jnp.exp(tops[k] - top)
        total = total + totals[k] * factor
        acc = acc + accs[k] * factor
    merged = acc / total
    row_ctx[...] = jnp.zeros((ROWS, HEADS * HEAD), F32)
    for j in range(HEADS):
        row_ctx[:LIVE, j * HEAD : (j + 1) * HEAD] = merged[j * LIVE : (j + 1) * LIVE]


def factor_body(ids, oth, ctx, row_ctx, down0, down1, own_out, oth_out):
    core = ids[CORE]
    parts = HEADS * HEAD // CHUNK
    rows = row_ctx[...].astype(BF16)

    def block(at, t):
        total = jnp.zeros((RANK, BLOCK), F32)
        for i in range(parts):
            total += nt(jnp.where(t == 1, down1[i, 0], down0[i, 0]), ctx[aligned(at, BLOCK), i * CHUNK : (i + 1) * CHUNK])
        return total.astype(BF16)

    row_terms = []
    for t in range(2):
        total = jnp.zeros((ROWS, RANK), F32)
        for i in range(parts):
            total += nt(rows[:, i * CHUNK : (i + 1) * CHUNK], (down0, down1)[t][i, 0])
        row_terms.append(total)
    row_part = jnp.where(row_mask(ids, ROWS, RANK), row_terms[1], row_terms[0]).astype(BF16)
    for out, at, t in ((own_out, core, ids[OWN]), (oth_out, 1 - core, oth[0])):
        out[:RANK, :] = block(at, t)
        out[RANK:, :] = jnp.zeros((ROWS, BLOCK), BF16)
        out[RANK:, :RANK] = row_part


def out_body(ids, a, b, up, own_up, out, row_out):
    total = a[...].astype(F32) + b[...].astype(F32)
    factor = jnp.transpose(total[:RANK]).astype(BF16)
    for i in range(2 * CHIPS):
        out[:, i * CHUNK : (i + 1) * CHUNK] = nn(factor, up[i, 0]).astype(BF16)
    rows = total[RANK:, :RANK].astype(BF16)
    terms = [nn(rows, own_up[t]) for t in range(2)]
    row_out[...] = jnp.where(row_mask(ids, ROWS, CHUNK), terms[1], terms[0])[:LIVE].astype(BF16)


def per_device(
    prompt_hidden,
    prompt_qkv,
    block_tenant,
    row_hidden,
    row_qkv,
    row_tenant,
    row_cache,
    row_lengths,
    qkv_down,
    qkv_up,
    out_down,
    out_up,
):
    blk = lax.axis_index("blk")
    role = lax.axis_index("role")
    chip, core = blk // 2, blk % 2
    head = 2 * role + core
    ids = jnp.concatenate(
        [
            jnp.stack([role, chip, core]).astype(jnp.int32),
            block_tenant,
            row_tenant,
            row_lengths,
            jnp.stack([head, 2 * role + 1 - core]).astype(jnp.int32),
        ]
    )

    def to_core(value):
        return lax.ppermute(value, "blk", [(i, i ^ 1) for i in range(2 * CHIPS)])

    def to_role(value):
        return lax.ppermute(value, "role", [(0, 1), (1, 0)])

    down = jnp.transpose(qkv_down, (0, 2, 1))
    downs = gather_chips(down)
    (mixed,) = call(
        pack_body,
        [ids],
        [qkv_up, jnp.transpose(out_down, (0, 2, 1)), out_up],
        [None] * 3,
        [shape((7, RANK, CHUNK))],
    )
    weights = lax.all_gather(mixed, "blk")
    oth = to_core(block_tenant)
    hid_oth, qkv_oth, cache_oth = to_core(prompt_hidden), to_core(prompt_qkv), to_core(row_cache)
    row_hid = jnp.pad(row_hidden, ((0, ROWS - LIVE), (0, 0)))
    row_base = jnp.pad(row_qkv, ((0, ROWS - LIVE), (0, 0)))

    (part,) = call(
        low_body,
        [ids, oth],
        [prompt_hidden, hid_oth, row_hid, *downs],
        [None] * (3 + CHIPS),
        [shape((2 * BLOCK + ROWS, 3 * RANK))],
    )
    mine = (part.astype(F32) + to_core(part).astype(F32)).astype(BF16)
    theirs = to_role(mine)

    columns = [
        spec((BLOCK, HEADS * HEAD), lambda s: (0, s[HEAD_ID])),
        spec((BLOCK, HEAD), lambda s: (0, 32 + s[HEAD_ID])),
        spec((BLOCK, HEAD), lambda s: (0, 36 + s[HEAD_ID])),
    ]
    row_columns = [
        spec((ROWS, HEADS * HEAD), lambda s: (0, s[HEAD_ID])),
        spec((ROWS, HEAD), lambda s: (0, 32 + s[HEAD_ID])),
        spec((ROWS, HEAD), lambda s: (0, 36 + s[HEAD_ID])),
    ]
    cached = [
        spec((LIVE - 1, BLOCK, HEAD), lambda s: (0, 0, s[HEAD_ID])),
        spec((LIVE - 1, BLOCK, HEAD), lambda s: (0, 0, 4 + s[HEAD_ID])),
    ]
    q, kv = call(
        proj_body,
        [ids, oth],
        [mine, theirs]
        + [prompt_qkv] * 3
        + [qkv_oth] * 3
        + [row_base] * 3
        + [row_cache] * 2
        + [cache_oth] * 2
        + [weights] * 3,
        [None, None]
        + columns
        + columns
        + row_columns
        + cached
        + cached
        + [spec((2 * CHIPS, 1, RANK, CHUNK), lambda s, i=i: (0, i, 0, 0)) for i in range(3)],
        [shape((2 * BLOCK, HEADS * HEAD)), shape((2 * BLOCK + HEADS * LIVE, 2 * HEAD))],
        [pltpu.VMEM((CHIPS, 2, RANK, 5 * HEAD), BF16)],
        48,
    )
    kvs = gather_chips(kv)
    ctx, row_ctx = call(
        attend_body,
        [ids],
        [q, *kvs],
        [None] * (1 + CHIPS),
        [shape((2 * BLOCK, HEADS * HEAD)), shape((ROWS, HEADS * HEAD), F32)],
        [pltpu.VMEM((CHIPS * 2 * BLOCK, HEAD), BF16), pltpu.VMEM((CHIPS * 2 * BLOCK, 2 * HEAD), BF16)],
        32,
    )
    own, other = call(
        factor_body,
        [ids, oth],
        [ctx, row_ctx, weights, weights],
        [None, None]
        + [spec((4, 1, RANK, CHUNK), lambda s, t=t: (s[HEAD_ID], 3 + t, 0, 0)) for t in range(2)],
        [shape((RANK + ROWS, BLOCK)), shape((RANK + ROWS, BLOCK))],
        limit=48,
    )
    mine = (own.astype(F32) + to_core(other).astype(F32)).astype(BF16)
    return tuple(
        call(
            out_body,
            [ids],
            [mine, to_role(mine), weights, out_up],
            [None, None, spec((2 * CHIPS, 1, RANK, CHUNK), lambda s: (0, 5 + s[OWN], 0, 0)), None],
            [shape(prompt_hidden.shape), shape((LIVE, CHUNK))],
            limit=48,
        )
    )


def solution(mesh):
    in_specs = (
        P(("grp", "blk"), "role"),
        P(("grp", "blk"), None),
        P(("grp", "blk")),
        P("grp", None),
        P("grp", None),
        P("grp"),
        P("grp", "blk", None),
        P("grp"),
        P(None, ("role", "blk"), None),
        P(None, None, "blk"),
        P(None, "blk", None),
        P(None, None, ("role", "blk")),
    )
    out_specs = (P(("grp", "blk"), "role"), P("grp", ("role", "blk")))
    return jax.shard_map(
        per_device, mesh=mesh, in_specs=in_specs, out_specs=out_specs, check_vma=False
    )
```

```python
import jax
import jax.numpy as jnp
from jax import lax
from jax.experimental import pallas as pl
from jax.experimental.pallas import tpu as pltpu
from jax.sharding import PartitionSpec as P

HEADS = 8
HEAD = 128
RANK = 64
BLOCK = 128
CHIPS = 8
CHUNK = 256
ROWS = 16
LIVE = 4
SCALE = HEAD ** -0.5
LOG2E = 1.4426950408889634
NEG = -1e30
F32 = jnp.float32
BF16 = jnp.bfloat16
MIB = 1 << 20

ROLE, CHIP, CORE, OWN, ROW_T, LENGTH, HEAD_ID, HEAD_OTHER, SCALARS = 0, 1, 2, 3, 4, 8, 11, 12, 13


def nt(a, b):
    return lax.dot_general(a, b, (((1,), (1,)), ((), ())), preferred_element_type=F32)


def nn(a, b):
    return jnp.dot(a, b, preferred_element_type=F32)


def aligned(index, size):
    return pl.ds(pl.multiple_of(index * size, size), size)


def call(body, scalars, args, in_specs, outs, scratch=(), limit=16, out_specs=None):
    def whole(shape):
        zeros = (0,) * len(shape)
        return pl.BlockSpec(shape, lambda i, *s: zeros)

    specs = [whole(a.shape) if spec is None else spec for a, spec in zip(args, in_specs)]
    return pl.pallas_call(
        body,
        grid_spec=pltpu.PrefetchScalarGridSpec(
            num_scalar_prefetch=len(scalars),
            grid=(1,),
            in_specs=specs,
            out_specs=out_specs or [whole(o.shape) for o in outs],
            scratch_shapes=list(scratch),
        ),
        out_shape=outs,
        compiler_params=pltpu.CompilerParams(vmem_limit_bytes=limit * MIB),
    )(*scalars, *args)


def spec(shape, place):
    return pl.BlockSpec(shape, lambda i, ids, *s: place(ids))


def shape(dims, dtype=BF16):
    return jax.ShapeDtypeStruct(dims, dtype)


STEPS = ((0, 0), (0, 1), (1, 0), (3, 0), (1, 1), (3, 1), (2, 0), (2, 1))


def source(chip, step):
    dy, dx = step
    return lax.rem(chip // 2 + dy, 4) * 2 + (lax.rem(chip, 2) ^ dx)


def gather_chips(value):
    def get(value, step):
        pairs = []
        for i in range(2 * CHIPS):
            y, x, core = i // 4, i // 2 % 2, i % 2
            pairs.append(((y + step[0]) % 4 * 4 + (x ^ step[1]) * 2 + core, i))
        return lax.ppermute(value, "blk", pairs)

    up = get(value, (1, 0))
    down_across = get(value, (3, 1))
    across = get(value, (0, 1))
    down = get(value, (3, 0))
    up_across = get(value, (1, 1))
    far = get(up, (1, 0))
    far_across = get(down_across, (3, 0))
    return [value, across, up, down, up_across, down_across, far, far_across]


def pack_body(place, up, down, out_up, out):
    def columns(main, tail, at):
        for t in range(2):
            out[t] = up[t, :, main : main + CHUNK]
            out[2, :, t * HEAD : (t + 1) * HEAD] = jnp.zeros((RANK, HEAD), BF16)
            out[2, :, t * HEAD + at : t * HEAD + at + RANK] = up[t, :, tail : tail + RANK]

    pl.when(lax.rem(place[0], 2) == 0)(lambda: columns(0, CHUNK, 0))
    pl.when(lax.rem(place[0], 2) == 1)(lambda: columns(RANK, 0, RANK))
    for t in range(2):
        out[3 + t] = down[t]
        out[5 + t] = out_up[t]


def hidden_body(place, adapter, hid, own, to_core, to_x, to_cross, tenant, sems):
    x, core = lax.rem(place[0] // 2, 2), lax.rem(place[0], 2)
    tenant[...] = jnp.full((ROWS, 4 * CHUNK), adapter[0].astype(F32)).astype(BF16)
    copies = []

    def move(src, dst):
        copies.append(pltpu.make_async_copy(src, dst, sems.at[len(copies)]))

    for out, dx, dc in ((own, 0, 0), (to_core, 0, 1), (to_x, 1, 0), (to_cross, 1, 1)):
        for y in range(4):
            chunk = 4 * y + 2 * (x ^ dx) + (core ^ dc)
            move(hid.at[:, aligned(chunk, CHUNK)], out.at[:BLOCK, y * CHUNK : (y + 1) * CHUNK])
        move(tenant, out.at[BLOCK:, :])
    for copy in copies:
        copy.start()
    for copy in copies:
        copy.wait()


CACHE_AT = (HEADS + 2) * HEAD
PACKED = CACHE_AT + (LIVE - 1) * 2 * HEAD


def base_body(ids, qkv, cache, own, other, sems):
    copies = []

    def move(src, out, at, width):
        copies.append(pltpu.make_async_copy(src, out.at[:, at : at + width], sems.at[len(copies)]))

    for out, head in ((own, ids[HEAD_ID]), (other, ids[HEAD_OTHER])):
        move(qkv.at[:, aligned(head, HEADS * HEAD)], out, 0, HEADS * HEAD)
        move(qkv.at[:, aligned(32 + head, HEAD)], out, HEADS * HEAD, HEAD)
        move(qkv.at[:, aligned(36 + head, HEAD)], out, (HEADS + 1) * HEAD, HEAD)
        for r in range(LIVE - 1):
            for half in range(2):
                at = CACHE_AT + (2 * r + half) * HEAD
                move(cache.at[r, :, aligned(4 * half + head, HEAD)], out, at, HEAD)
    for copy in copies:
        copy.start()
    for copy in copies:
        copy.wait()


LOW_ROWS = 3 * BLOCK + 2 * ROWS


def low_body(ids, own, by_core, by_x, by_cross, row_hid, w0, w1, w3, w2, mine, theirs):
    role, y, x, core = ids[ROLE], ids[CHIP] // 2, lax.rem(ids[CHIP], 2), ids[CORE]
    sums = [[jnp.zeros((n, 3 * RANK), F32) for _ in range(2)] for n in (BLOCK, BLOCK, BLOCK, BLOCK, ROWS)]
    for dy, w in ((0, w0), (1, w1), (3, w3), (2, w2)):
        src = lax.rem(y + dy, 4)
        parts = [hid[:BLOCK, aligned(src, CHUNK)] for hid in (own, by_core, by_x, by_cross)]
        parts.append(row_hid[:, aligned(role * 2 * CHIPS + 4 * src + 2 * x + core, CHUNK)])
        for total, part in zip(sums, parts):
            for t in range(2):
                total[t] += nt(part, w[t])

    def chosen(at, hid):
        adapter = jnp.broadcast_to(hid[BLOCK : BLOCK + 1, : 3 * RANK].astype(F32), (BLOCK, 3 * RANK))
        return jnp.where(adapter > 0.5, sums[at][1], sums[at][0])

    rows = jnp.where(row_mask(ids, ROWS, 3 * RANK), sums[4][1], sums[4][0]).astype(BF16)
    for out, (first, one), (second, two) in (
        (mine, (0, own), (1, by_core)),
        (theirs, (2, by_x), (3, by_cross)),
    ):
        first, second = chosen(first, one), chosen(second, two)
        even, odd = jnp.where(core == 0, first, second), jnp.where(core == 0, second, first)
        out[:BLOCK, :] = even[:, :HEAD].astype(BF16)
        out[BLOCK : 2 * BLOCK, :] = odd[:, :HEAD].astype(BF16)
        out[2 * BLOCK : 3 * BLOCK, :] = jnp.concatenate([even[:, HEAD:], odd[:, HEAD:]], axis=1).astype(BF16)
        out[3 * BLOCK : 3 * BLOCK + ROWS, :] = rows[:, :HEAD]
        out[3 * BLOCK + ROWS :, :RANK] = rows[:, HEAD:]
        out[3 * BLOCK + ROWS :, RANK:] = jnp.zeros((ROWS, RANK), BF16)


def row_mask(ids, rows, width):
    at = lax.broadcasted_iota(jnp.int32, (rows, width), 0)
    mask = jnp.zeros((rows, width), jnp.int32)
    for r in range(LIVE):
        mask = jnp.where(at == r, ids[ROW_T + r], mask)
    return mask == 1


def split3(x):
    hi = x.astype(BF16).astype(F32)
    mid = (x - hi).astype(BF16).astype(F32)
    return hi, mid, x - hi - mid


def cached(r, half):
    at = CACHE_AT + (2 * r + half) * HEAD
    return slice(at, at + HEAD)


def proj_body(
    ids, oth, mine, theirs, base, base_oth, rq, rk, rv, up0, up1, tail, q_out, kv_out, upb
):
    chip, core, head = ids[CHIP], ids[CORE], ids[HEAD_ID]
    for src in range(CHIPS):
        for t, up in enumerate((up0, up1)):
            lanes = slice(t * HEAD, (t + 1) * HEAD)
            upb[src, t, :, : 2 * HEAD] = up[2 * src, 0]
            upb[src, t, :, 2 * HEAD : 3 * HEAD] = tail[2 * src, 0, :, lanes] + tail[2 * src + 1, 0, :, lanes]
            upb[src, t, :, 3 * HEAD :] = up[2 * src + 1, 0]
    own_rows, oth_rows = aligned(core, BLOCK), aligned(1 - core, BLOCK)

    def low(rows):
        return (mine[rows, :].astype(F32) + theirs[rows, :].astype(F32)).astype(BF16)

    third = low(slice(2 * BLOCK, 3 * BLOCK))
    thirds = third[:, :RANK], third[:, RANK:]
    low_own = jnp.concatenate([low(own_rows), jnp.where(core == 0, *thirds)], axis=1)
    low_oth = jnp.concatenate([low(oth_rows), jnp.where(core == 1, *thirds)], axis=1)
    low_row = jnp.concatenate(
        [low(slice(3 * BLOCK, 3 * BLOCK + ROWS)), low(slice(3 * BLOCK + ROWS, LOW_ROWS))[:, :RANK]], axis=1
    )
    mask = row_mask(ids, ROWS, HEAD)
    row_q = []
    new_k = new_v = k_own = k_oth = v_own = v_oth = None
    for j in range(HEADS + 2):
        group = max(j - HEADS + 1, 0)
        tile = head * HEADS + j if j < HEADS else head + (32 if j == HEADS else 36)
        src, off = lax.div(tile, 5), lax.rem(tile, 5)
        columns = aligned(off, HEAD)
        part = slice(group * RANK, (group + 1) * RANK)
        here = slice(j * HEAD, (j + 1) * HEAD)
        row_base = (rq[:, here] if j < HEADS else (rk if j == HEADS else rv)[...]).astype(F32)
        got_own = (base[:, here].astype(F32) + nn(low_own[:, part], upb[src, ids[OWN], :, columns])).astype(BF16)
        got_oth = (base_oth[:, here].astype(F32) + nn(low_oth[:, part], upb[src, oth[0], :, columns])).astype(BF16)
        row_terms = [nn(low_row[:, part], upb[src, t, :, columns]) for t in range(2)]
        got_row = (row_base + jnp.where(mask, row_terms[1], row_terms[0])).astype(BF16)
        if j < HEADS:
            q_out[own_rows, here] = got_own
            q_out[oth_rows, here] = got_oth
            row_q.append(got_row)
        elif j == HEADS:
            kv_out[own_rows, :HEAD] = got_own
            kv_out[oth_rows, :HEAD] = got_oth
            k_own, k_oth, new_k = got_own, got_oth, got_row
        else:
            kv_out[own_rows, HEAD:] = got_own
            kv_out[oth_rows, HEAD:] = got_oth
            v_own, v_oth, new_v = got_own, got_oth, got_row

    count = HEADS * ROWS
    queries = jnp.concatenate(row_q, axis=0)
    row_id = lax.rem(lax.broadcasted_iota(jnp.int32, (count, BLOCK), 0), ROWS)
    lane = lax.broadcasted_iota(jnp.int32, (count, BLOCK), 1)
    halves = []
    for at, first in ((core, 0), (1 - core, 1)):
        scores = nt(queries, k_oth if first else k_own)
        valid = jnp.full((count, BLOCK), 1, jnp.int32)
        position = (2 * chip + at) * BLOCK + lane
        for r in range(LIVE - 1):
            keys = (base_oth if first else base)[:, cached(r, 0)]
            this = row_id == r + 1
            scores = jnp.where(this, nt(queries, keys), scores)
            valid = jnp.where(this, (position < ids[LENGTH + r]).astype(jnp.int32), valid)
        halves.append((jnp.where(valid == 1, scores * SCALE, NEG), valid == 1))
    own_lane = lax.broadcasted_iota(jnp.int32, (count, ROWS), 1)
    own_row = lax.rem(lax.broadcasted_iota(jnp.int32, (count, ROWS), 0), ROWS)
    first_chip = chip == 0
    own_score = jnp.where((own_lane == own_row) & first_chip, nt(queries, new_k) * SCALE, NEG)
    top = jnp.max(jnp.maximum(halves[0][0], halves[1][0]), axis=1, keepdims=True)
    top = jnp.maximum(top, jnp.max(own_score, axis=1, keepdims=True))
    own_weight = jnp.where((own_lane == own_row) & first_chip, jnp.exp(own_score - top), 0.0)
    total = jnp.sum(own_weight, axis=1, keepdims=True)
    acc = nn(own_weight.astype(BF16), new_v)
    for first, (scores, valid) in enumerate(halves):
        weights = jnp.where(valid, jnp.exp(scores - top), 0.0)
        total = total + jnp.sum(weights, axis=1, keepdims=True)
        for r in range(LIVE):
            if r == 0:
                values = v_oth if first else v_own
            else:
                values = (base_oth if first else base)[:, cached(r - 1, 1)]
            acc = acc + nn(jnp.where(row_id == r, weights, 0.0).astype(BF16), values)
    stats = jnp.zeros((count, HEAD), F32)
    for place, value in enumerate(split3(top) + split3(total)):
        stats = jnp.where(lane // 16 == place, value, stats)
    keep_row = lax.broadcasted_iota(jnp.int32, (HEADS * LIVE, count), 0)
    keep_from = lax.broadcasted_iota(jnp.int32, (HEADS * LIVE, count), 1)
    keep = jnp.where((keep_row // LIVE) * ROWS + keep_row % LIVE == keep_from, 1.0, 0.0).astype(BF16)
    kv_out[2 * BLOCK :, :HEAD] = nn(keep, acc.astype(BF16)).astype(BF16)
    kv_out[2 * BLOCK :, HEAD:] = nn(keep, stats.astype(BF16)).astype(BF16)


def attend_body(ids, q, *rest):
    kvs, (ctx, row_ctx), (keys, values) = rest[:CHIPS], rest[CHIPS : CHIPS + 2], rest[CHIPS + 2 :]
    chip = ids[CHIP]
    span = 2 * BLOCK
    values[:, HEAD:] = jnp.ones((CHIPS * span, HEAD), BF16)
    for k in range(CHIPS):
        keys[aligned(source(chip, STEPS[k]), span), :] = kvs[k][:span, :HEAD]
        values[aligned(source(chip, STEPS[k]), span), :HEAD] = kvs[k][:span, HEAD:]

    def branch(chips):
        below, tail = (chips - 2) * span, 2 * span

        def head_scores(j):
            queries = q[:, aligned(j, HEAD)]
            last = nt(queries, keys[below : below + tail, :])
            row = lax.broadcasted_iota(jnp.int32, (span, tail), 0) + (chip - (chips - 2)) * span
            col = lax.broadcasted_iota(jnp.int32, (span, tail), 1)
            scores = [jnp.where(col <= row, last, NEG)]
            if below:
                scores.append(nt(queries, keys[:below, :]))
            return scores

        def head_context(j, scores):
            top = jnp.max(scores[0], axis=1, keepdims=True)
            if below:
                top = jnp.maximum(top, jnp.max(scores[1], axis=1, keepdims=True))
            acc = 0.0
            for score, rows in zip(scores, (slice(below, below + tail), slice(0, below))):
                weights = jnp.exp2((score - top) * (SCALE * LOG2E)).astype(BF16)
                acc = acc + nn(weights, values[rows, :])
            ctx[:, aligned(j, HEAD)] = (acc[:, :HEAD] / acc[:, HEAD:]).astype(BF16)

        def two_heads(i, carry):
            scores = [head_scores(2 * i + e) for e in range(2)]
            for e in range(2):
                head_context(2 * i + e, scores[e])
            return carry

        lax.fori_loop(0, HEADS // 2, two_heads, 0)

    for chips in range(2, CHIPS + 1, 2):
        pl.when(chip // 2 == chips // 2 - 1)(lambda chips=chips: branch(chips))

    tops, totals, accs = [], [], []
    for k in range(CHIPS):
        stats = kvs[k][span:, HEAD:].astype(F32)
        tops.append(stats[:, 0:1] + stats[:, 16:17] + stats[:, 32:33])
        totals.append(stats[:, 48:49] + stats[:, 64:65] + stats[:, 80:81])
        accs.append(kvs[k][span:, :HEAD].astype(F32))
    top = tops[0]
    for value in tops[1:]:
        top = jnp.maximum(top, value)
    total, acc = 0.0, 0.0
    for k in range(CHIPS):
        factor = jnp.exp(tops[k] - top)
        total = total + totals[k] * factor
        acc = acc + accs[k] * factor
    merged = acc / total
    row_ctx[...] = jnp.zeros((ROWS, HEADS * HEAD), F32)
    for j in range(HEADS):
        row_ctx[:LIVE, j * HEAD : (j + 1) * HEAD] = merged[j * LIVE : (j + 1) * LIVE]


def factor_body(ids, oth, ctx, row_ctx, down0, down1, own_out, oth_out):
    core = ids[CORE]
    parts = HEADS * HEAD // CHUNK
    rows = row_ctx[...].astype(BF16)

    def block(at, t):
        total = jnp.zeros((RANK, BLOCK), F32)
        for i in range(parts):
            total += nt(jnp.where(t == 1, down1[i, 0], down0[i, 0]), ctx[aligned(at, BLOCK), i * CHUNK : (i + 1) * CHUNK])
        return total.astype(BF16)

    row_terms = []
    for t in range(2):
        total = jnp.zeros((ROWS, RANK), F32)
        for i in range(parts):
            total += nt(rows[:, i * CHUNK : (i + 1) * CHUNK], (down0, down1)[t][i, 0])
        row_terms.append(total)
    row_part = jnp.where(row_mask(ids, ROWS, RANK), row_terms[1], row_terms[0]).astype(BF16)
    for out, at, t in ((own_out, core, ids[OWN]), (oth_out, 1 - core, oth[0])):
        out[:RANK, :] = block(at, t)
        out[RANK:, :] = jnp.zeros((ROWS, BLOCK), BF16)
        out[RANK:, :RANK] = row_part


def out_body(ids, a, b, up, own_up, out, row_out):
    total = a[...].astype(F32) + b[...].astype(F32)
    factor = jnp.transpose(total[:RANK]).astype(BF16)
    for i in range(2 * CHIPS):
        out[:, i * CHUNK : (i + 1) * CHUNK] = nn(factor, up[i, 0]).astype(BF16)
    rows = total[RANK:, :RANK].astype(BF16)
    terms = [nn(rows, own_up[t]) for t in range(2)]
    row_out[...] = jnp.where(row_mask(ids, ROWS, CHUNK), terms[1], terms[0])[:LIVE].astype(BF16)


def per_device(
    prompt_hidden,
    prompt_qkv,
    block_tenant,
    row_hidden,
    row_qkv,
    row_tenant,
    row_cache,
    row_lengths,
    qkv_down,
    qkv_up,
    out_down,
    out_up,
):
    blk = lax.axis_index("blk")
    role = lax.axis_index("role")
    chip, core = blk // 2, blk % 2
    head = 2 * role + core
    ids = jnp.concatenate(
        [
            jnp.stack([role, chip, core]).astype(jnp.int32),
            block_tenant,
            row_tenant,
            row_lengths,
            jnp.stack([head, 2 * role + 1 - core]).astype(jnp.int32),
        ]
    )

    def to_core(value):
        return lax.ppermute(value, "blk", [(i, i ^ 1) for i in range(2 * CHIPS)])

    def to_role(value):
        return lax.ppermute(value, "role", [(0, 1), (1, 0)])

    down = jnp.transpose(qkv_down, (0, 2, 1))
    def to_x(value):
        return lax.ppermute(value, "blk", [(i, i ^ 2) for i in range(2 * CHIPS)])

    def from_row(value, dy):
        pairs = [((i + 4 * dy) % (2 * CHIPS), i) for i in range(2 * CHIPS)]
        return lax.ppermute(value, "blk", pairs)

    place = jnp.reshape(blk, (1,))
    (weights,) = call(
        pack_body,
        [place],
        [qkv_up, jnp.transpose(out_down, (0, 2, 1)), out_up],
        [None] * 3,
        [shape((7, RANK, CHUNK))],
        limit=48,
    )
    weights = lax.all_gather(weights, "blk")
    arrived = from_row(down, 1)
    downs = [down, arrived, from_row(down, 3), from_row(down, 2)]
    hid, core_hid, x_hid, cross_hid = call(
        hidden_body,
        [place, block_tenant],
        [prompt_hidden],
        [pl.BlockSpec(memory_space=pl.ANY)],
        [shape((BLOCK + ROWS, 4 * CHUNK))] * 4,
        [pltpu.VMEM((ROWS, 4 * CHUNK), BF16), pltpu.SemaphoreType.DMA((20,))],
        48,
        out_specs=[pl.BlockSpec(memory_space=pl.ANY)] * 4,
    )
    cross_hid = lax.ppermute(cross_hid, "blk", [(i, i ^ 3) for i in range(2 * CHIPS)])
    x_hid, core_hid = to_x(x_hid), to_core(core_hid)
    base, base_send = call(
        base_body,
        [lax.optimization_barrier((ids, arrived))[0]],
        [prompt_qkv, row_cache],
        [pl.BlockSpec(memory_space=pl.ANY)] * 2,
        [shape((BLOCK, PACKED))] * 2,
        [pltpu.SemaphoreType.DMA((2 * (3 + 2 * (LIVE - 1)),))],
        48,
        out_specs=[pl.BlockSpec(memory_space=pl.ANY)] * 2,
    )
    base_oth = to_core(base_send)
    oth = to_core(block_tenant)
    row_hid = jnp.pad(row_hidden, ((0, ROWS - LIVE), (0, 0)))
    row_base = jnp.pad(row_qkv, ((0, ROWS - LIVE), (0, 0)))

    part, part_x = call(
        low_body,
        [ids],
        [hid, core_hid, x_hid, cross_hid, row_hid, *downs],
        [None] * 9,
        [shape((LOW_ROWS, HEAD))] * 2,
    )
    mine = (part.astype(F32) + to_x(part_x).astype(F32)).astype(BF16)
    mine = (mine.astype(F32) + to_core(mine).astype(F32)).astype(BF16)
    theirs = to_role(mine)
    row_columns = [
        spec((ROWS, HEADS * HEAD), lambda s: (0, s[HEAD_ID])),
        spec((ROWS, HEAD), lambda s: (0, 32 + s[HEAD_ID])),
        spec((ROWS, HEAD), lambda s: (0, 36 + s[HEAD_ID])),
    ]
    q, kv = call(
        proj_body,
        [ids, oth],
        [mine, theirs, base, base_oth] + [row_base] * 3 + [weights] * 3,
        [None] * 4
        + row_columns
        + [spec((2 * CHIPS, 1, RANK, CHUNK), lambda s, i=i: (0, i, 0, 0)) for i in range(3)],
        [shape((2 * BLOCK, HEADS * HEAD)), shape((2 * BLOCK + HEADS * LIVE, 2 * HEAD))],
        [pltpu.VMEM((CHIPS, 2, RANK, 5 * HEAD), BF16)],
        48,
    )
    kvs = gather_chips(kv)
    ctx, row_ctx = call(
        attend_body,
        [ids],
        [q, *kvs],
        [None] * (1 + CHIPS),
        [shape((2 * BLOCK, HEADS * HEAD)), shape((ROWS, HEADS * HEAD), F32)],
        [pltpu.VMEM((CHIPS * 2 * BLOCK, HEAD), BF16), pltpu.VMEM((CHIPS * 2 * BLOCK, 2 * HEAD), BF16)],
        32,
    )
    own, other = call(
        factor_body,
        [ids, oth],
        [ctx, row_ctx, weights, weights],
        [None, None]
        + [spec((4, 1, RANK, CHUNK), lambda s, t=t: (s[HEAD_ID], 3 + t, 0, 0)) for t in range(2)],
        [shape((RANK + ROWS, BLOCK)), shape((RANK + ROWS, BLOCK))],
        limit=48,
    )
    mine = (own.astype(F32) + to_core(other).astype(F32)).astype(BF16)
    return tuple(
        call(
            out_body,
            [ids],
            [mine, to_role(mine), weights, out_up],
            [None, None, spec((2 * CHIPS, 1, RANK, CHUNK), lambda s: (0, 5 + s[OWN], 0, 0)), None],
            [shape(prompt_hidden.shape), shape((LIVE, CHUNK))],
            limit=48,
        )
    )


def solution(mesh):
    in_specs = (
        P(("grp", "blk"), "role"),
        P(("grp", "blk"), None),
        P(("grp", "blk")),
        P("grp", None),
        P("grp", None),
        P("grp"),
        P("grp", "blk", None),
        P("grp"),
        P(None, ("role", "blk"), None),
        P(None, None, "blk"),
        P(None, "blk", None),
        P(None, None, ("role", "blk")),
    )
    out_specs = (P(("grp", "blk"), "role"), P("grp", ("role", "blk")))
    return jax.shard_map(
        per_device, mesh=mesh, in_specs=in_specs, out_specs=out_specs, check_vma=False
    )
```

```python
import jax
import jax.numpy as jnp
from jax import lax
from jax.experimental import pallas as pl
from jax.experimental.pallas import tpu as pltpu
from jax.sharding import PartitionSpec as P

HEADS = 8
HEAD = 128
RANK = 64
BLOCK = 128
CHIPS = 8
CHUNK = 256
ROWS = 16
LIVE = 4
SCALE = HEAD ** -0.5
LOG2E = 1.4426950408889634
NEG = -1e30
F32 = jnp.float32
BF16 = jnp.bfloat16
MIB = 1 << 20

ROLE, CHIP, CORE, OWN, ROW_T, LENGTH, HEAD_ID, HEAD_OTHER, SCALARS = 0, 1, 2, 3, 4, 8, 11, 12, 13


def nt(a, b):
    return lax.dot_general(a, b, (((1,), (1,)), ((), ())), preferred_element_type=F32)


def nn(a, b):
    return jnp.dot(a, b, preferred_element_type=F32)


def aligned(index, size):
    return pl.ds(pl.multiple_of(index * size, size), size)


def call(body, scalars, args, in_specs, outs, scratch=(), limit=16, out_specs=None):
    def whole(shape):
        zeros = (0,) * len(shape)
        return pl.BlockSpec(shape, lambda i, *s: zeros)

    specs = [whole(a.shape) if spec is None else spec for a, spec in zip(args, in_specs)]
    return pl.pallas_call(
        body,
        grid_spec=pltpu.PrefetchScalarGridSpec(
            num_scalar_prefetch=len(scalars),
            grid=(1,),
            in_specs=specs,
            out_specs=out_specs or [whole(o.shape) for o in outs],
            scratch_shapes=list(scratch),
        ),
        out_shape=outs,
        compiler_params=pltpu.CompilerParams(vmem_limit_bytes=limit * MIB),
    )(*scalars, *args)


def spec(shape, place):
    return pl.BlockSpec(shape, lambda i, ids, *s: place(ids))


def shape(dims, dtype=BF16):
    return jax.ShapeDtypeStruct(dims, dtype)


STEPS = ((0, 0), (0, 1), (1, 0), (3, 0), (1, 1), (3, 1), (2, 0), (2, 1))


def source(chip, step):
    dy, dx = step
    return lax.rem(chip // 2 + dy, 4) * 2 + (lax.rem(chip, 2) ^ dx)


def gather_chips(value):
    def get(value, step):
        pairs = []
        for i in range(2 * CHIPS):
            y, x, core = i // 4, i // 2 % 2, i % 2
            pairs.append(((y + step[0]) % 4 * 4 + (x ^ step[1]) * 2 + core, i))
        return lax.ppermute(value, "blk", pairs)

    up = get(value, (1, 0))
    down_across = get(value, (3, 1))
    across = get(value, (0, 1))
    down = get(value, (3, 0))
    up_across = get(value, (1, 1))
    far = get(up, (1, 0))
    far_across = get(down_across, (3, 0))
    return [value, across, up, down, up_across, down_across, far, far_across]


SNAKE = [4 * y + 2 * (i ^ (y % 2)) + core for y in range(4) for i in range(2) for core in range(2)]


def pack_body(place, up, down, out_up, out):
    def columns(main, tail, at):
        for t in range(2):
            out[t] = up[t, :, main : main + CHUNK]
            out[2, :, t * HEAD : (t + 1) * HEAD] = jnp.zeros((RANK, HEAD), BF16)
            out[2, :, t * HEAD + at : t * HEAD + at + RANK] = up[t, :, tail : tail + RANK]

    pl.when(lax.rem(place[0], 2) == 0)(lambda: columns(0, CHUNK, 0))
    pl.when(lax.rem(place[0], 2) == 1)(lambda: columns(RANK, 0, RANK))
    for t in range(2):
        out[3 + t] = down[t]
        out[5 + t] = out_up[t]


def hidden_body(place, adapter, hid, own, to_core, to_x, to_cross, tenant, sems):
    x, core = lax.rem(place[0] // 2, 2), lax.rem(place[0], 2)
    tenant[...] = jnp.full((ROWS, 4 * CHUNK), adapter[0].astype(F32)).astype(BF16)
    copies = []

    def move(src, dst):
        copies.append(pltpu.make_async_copy(src, dst, sems.at[len(copies)]))

    for out, dx, dc in ((own, 0, 0), (to_core, 0, 1), (to_x, 1, 0), (to_cross, 1, 1)):
        for y in range(4):
            chunk = 4 * y + 2 * (x ^ dx) + (core ^ dc)
            move(hid.at[:, aligned(chunk, CHUNK)], out.at[:BLOCK, y * CHUNK : (y + 1) * CHUNK])
        move(tenant, out.at[BLOCK:, :])
    for copy in copies:
        copy.start()
    for copy in copies:
        copy.wait()


CACHE_AT = (HEADS + 2) * HEAD
PACKED = CACHE_AT + (LIVE - 1) * 2 * HEAD


def base_body(ids, qkv, cache, own, other, sems):
    copies = []

    def move(src, out, at, width):
        copies.append(pltpu.make_async_copy(src, out.at[:, at : at + width], sems.at[len(copies)]))

    for out, head in ((own, ids[HEAD_ID]), (other, ids[HEAD_OTHER])):
        move(qkv.at[:, aligned(head, HEADS * HEAD)], out, 0, HEADS * HEAD)
        move(qkv.at[:, aligned(32 + head, HEAD)], out, HEADS * HEAD, HEAD)
        move(qkv.at[:, aligned(36 + head, HEAD)], out, (HEADS + 1) * HEAD, HEAD)
        for r in range(LIVE - 1):
            for half in range(2):
                at = CACHE_AT + (2 * r + half) * HEAD
                move(cache.at[r, :, aligned(4 * half + head, HEAD)], out, at, HEAD)
    for copy in copies:
        copy.start()
    for copy in copies:
        copy.wait()


LOW_ROWS = 3 * BLOCK + 2 * ROWS


def low_body(ids, own, by_core, by_x, by_cross, row_hid, w0, w1, w3, w2, mine, theirs):
    role, y, x, core = ids[ROLE], ids[CHIP] // 2, lax.rem(ids[CHIP], 2), ids[CORE]
    sums = [[jnp.zeros((n, 3 * RANK), F32) for _ in range(2)] for n in (BLOCK, BLOCK, BLOCK, BLOCK, ROWS)]
    for dy, w in ((0, w0), (1, w1), (3, w3), (2, w2)):
        src = lax.rem(y + dy, 4)
        parts = [hid[:BLOCK, aligned(src, CHUNK)] for hid in (own, by_core, by_x, by_cross)]
        parts.append(row_hid[:, aligned(role * 2 * CHIPS + 4 * src + 2 * x + core, CHUNK)])
        for total, part in zip(sums, parts):
            for t in range(2):
                total[t] += nt(part, w[t])

    def chosen(at, hid):
        adapter = jnp.broadcast_to(hid[BLOCK : BLOCK + 1, : 3 * RANK].astype(F32), (BLOCK, 3 * RANK))
        return jnp.where(adapter > 0.5, sums[at][1], sums[at][0])

    rows = jnp.where(row_mask(ids, ROWS, 3 * RANK), sums[4][1], sums[4][0]).astype(BF16)
    for out, (first, one), (second, two) in (
        (mine, (0, own), (1, by_core)),
        (theirs, (2, by_x), (3, by_cross)),
    ):
        first, second = chosen(first, one), chosen(second, two)
        even, odd = jnp.where(core == 0, first, second), jnp.where(core == 0, second, first)
        out[:BLOCK, :] = even[:, :HEAD].astype(BF16)
        out[BLOCK : 2 * BLOCK, :] = odd[:, :HEAD].astype(BF16)
        out[2 * BLOCK : 3 * BLOCK, :] = jnp.concatenate([even[:, HEAD:], odd[:, HEAD:]], axis=1).astype(BF16)
        out[3 * BLOCK : 3 * BLOCK + ROWS, :] = rows[:, :HEAD]
        out[3 * BLOCK + ROWS :, :RANK] = rows[:, HEAD:]
        out[3 * BLOCK + ROWS :, RANK:] = jnp.zeros((ROWS, RANK), BF16)


def row_mask(ids, rows, width):
    at = lax.broadcasted_iota(jnp.int32, (rows, width), 0)
    mask = jnp.zeros((rows, width), jnp.int32)
    for r in range(LIVE):
        mask = jnp.where(at == r, ids[ROW_T + r], mask)
    return mask == 1


def split3(x):
    hi = x.astype(BF16).astype(F32)
    mid = (x - hi).astype(BF16).astype(F32)
    return hi, mid, x - hi - mid


def cached(r, half):
    at = CACHE_AT + (2 * r + half) * HEAD
    return slice(at, at + HEAD)


def proj_body(
    ids, oth, mine, theirs, base, base_oth, rq, rk, rv, up0, up1, tail, q_out, kv_out, upb
):
    chip, core, head = ids[CHIP], ids[CORE], ids[HEAD_ID]
    for src in range(CHIPS):
        even, odd = SNAKE.index(2 * src), SNAKE.index(2 * src + 1)
        for t, up in enumerate((up0, up1)):
            lanes = slice(t * HEAD, (t + 1) * HEAD)
            upb[src, t, :, : 2 * HEAD] = up[even, 0]
            upb[src, t, :, 2 * HEAD : 3 * HEAD] = tail[even, 0, :, lanes] + tail[odd, 0, :, lanes]
            upb[src, t, :, 3 * HEAD :] = up[odd, 0]
    own_rows, oth_rows = aligned(core, BLOCK), aligned(1 - core, BLOCK)

    def low(rows):
        return (mine[rows, :].astype(F32) + theirs[rows, :].astype(F32)).astype(BF16)

    third = low(slice(2 * BLOCK, 3 * BLOCK))
    thirds = third[:, :RANK], third[:, RANK:]
    low_own = jnp.concatenate([low(own_rows), jnp.where(core == 0, *thirds)], axis=1)
    low_oth = jnp.concatenate([low(oth_rows), jnp.where(core == 1, *thirds)], axis=1)
    low_row = jnp.concatenate(
        [low(slice(3 * BLOCK, 3 * BLOCK + ROWS)), low(slice(3 * BLOCK + ROWS, LOW_ROWS))[:, :RANK]], axis=1
    )
    mask = row_mask(ids, ROWS, HEAD)
    row_q = []
    new_k = new_v = k_own = k_oth = v_own = v_oth = None
    for j in range(HEADS + 2):
        group = max(j - HEADS + 1, 0)
        tile = head * HEADS + j if j < HEADS else head + (32 if j == HEADS else 36)
        src, off = lax.div(tile, 5), lax.rem(tile, 5)
        columns = aligned(off, HEAD)
        part = slice(group * RANK, (group + 1) * RANK)
        here = slice(j * HEAD, (j + 1) * HEAD)
        row_base = (rq[:, here] if j < HEADS else (rk if j == HEADS else rv)[...]).astype(F32)
        got_own = (base[:, here].astype(F32) + nn(low_own[:, part], upb[src, ids[OWN], :, columns])).astype(BF16)
        got_oth = (base_oth[:, here].astype(F32) + nn(low_oth[:, part], upb[src, oth[0], :, columns])).astype(BF16)
        row_terms = [nn(low_row[:, part], upb[src, t, :, columns]) for t in range(2)]
        got_row = (row_base + jnp.where(mask, row_terms[1], row_terms[0])).astype(BF16)
        if j < HEADS:
            q_out[own_rows, here] = got_own
            q_out[oth_rows, here] = got_oth
            row_q.append(got_row)
        elif j == HEADS:
            kv_out[own_rows, :HEAD] = got_own
            kv_out[oth_rows, :HEAD] = got_oth
            k_own, k_oth, new_k = got_own, got_oth, got_row
        else:
            kv_out[own_rows, HEAD:] = got_own
            kv_out[oth_rows, HEAD:] = got_oth
            v_own, v_oth, new_v = got_own, got_oth, got_row

    count = HEADS * ROWS
    queries = jnp.concatenate(row_q, axis=0)
    row_id = lax.rem(lax.broadcasted_iota(jnp.int32, (count, BLOCK), 0), ROWS)
    lane = lax.broadcasted_iota(jnp.int32, (count, BLOCK), 1)
    halves = []
    for at, first in ((core, 0), (1 - core, 1)):
        scores = nt(queries, k_oth if first else k_own)
        valid = jnp.full((count, BLOCK), 1, jnp.int32)
        position = (2 * chip + at) * BLOCK + lane
        for r in range(LIVE - 1):
            keys = (base_oth if first else base)[:, cached(r, 0)]
            this = row_id == r + 1
            scores = jnp.where(this, nt(queries, keys), scores)
            valid = jnp.where(this, (position < ids[LENGTH + r]).astype(jnp.int32), valid)
        halves.append((jnp.where(valid == 1, scores * SCALE, NEG), valid == 1))
    own_lane = lax.broadcasted_iota(jnp.int32, (count, ROWS), 1)
    own_row = lax.rem(lax.broadcasted_iota(jnp.int32, (count, ROWS), 0), ROWS)
    first_chip = chip == 0
    own_score = jnp.where((own_lane == own_row) & first_chip, nt(queries, new_k) * SCALE, NEG)
    top = jnp.max(jnp.maximum(halves[0][0], halves[1][0]), axis=1, keepdims=True)
    top = jnp.maximum(top, jnp.max(own_score, axis=1, keepdims=True))
    own_weight = jnp.where((own_lane == own_row) & first_chip, jnp.exp(own_score - top), 0.0)
    total = jnp.sum(own_weight, axis=1, keepdims=True)
    acc = nn(own_weight.astype(BF16), new_v)
    for first, (scores, valid) in enumerate(halves):
        weights = jnp.where(valid, jnp.exp(scores - top), 0.0)
        total = total + jnp.sum(weights, axis=1, keepdims=True)
        for r in range(LIVE):
            if r == 0:
                values = v_oth if first else v_own
            else:
                values = (base_oth if first else base)[:, cached(r - 1, 1)]
            acc = acc + nn(jnp.where(row_id == r, weights, 0.0).astype(BF16), values)
    stats = jnp.zeros((count, HEAD), F32)
    for place, value in enumerate(split3(top) + split3(total)):
        stats = jnp.where(lane // 16 == place, value, stats)
    keep_row = lax.broadcasted_iota(jnp.int32, (HEADS * LIVE, count), 0)
    keep_from = lax.broadcasted_iota(jnp.int32, (HEADS * LIVE, count), 1)
    keep = jnp.where((keep_row // LIVE) * ROWS + keep_row % LIVE == keep_from, 1.0, 0.0).astype(BF16)
    kv_out[2 * BLOCK :, :HEAD] = nn(keep, acc.astype(BF16)).astype(BF16)
    kv_out[2 * BLOCK :, HEAD:] = nn(keep, stats.astype(BF16)).astype(BF16)


def attend_body(ids, q, *rest):
    kvs, (ctx, row_ctx), (keys, values) = rest[:CHIPS], rest[CHIPS : CHIPS + 2], rest[CHIPS + 2 :]
    chip = ids[CHIP]
    span = 2 * BLOCK
    values[:, HEAD:] = jnp.ones((CHIPS * span, HEAD), BF16)
    for k in range(CHIPS):
        keys[aligned(source(chip, STEPS[k]), span), :] = kvs[k][:span, :HEAD]
        values[aligned(source(chip, STEPS[k]), span), :HEAD] = kvs[k][:span, HEAD:]

    def branch(chips):
        below, tail = (chips - 2) * span, 2 * span

        def head_scores(j):
            queries = q[:, aligned(j, HEAD)]
            last = nt(queries, keys[below : below + tail, :])
            row = lax.broadcasted_iota(jnp.int32, (span, tail), 0) + (chip - (chips - 2)) * span
            col = lax.broadcasted_iota(jnp.int32, (span, tail), 1)
            scores = [jnp.where(col <= row, last, NEG)]
            if below:
                scores.append(nt(queries, keys[:below, :]))
            return scores

        def head_context(j, scores):
            top = jnp.max(scores[0], axis=1, keepdims=True)
            if below:
                top = jnp.maximum(top, jnp.max(scores[1], axis=1, keepdims=True))
            acc = 0.0
            for score, rows in zip(scores, (slice(below, below + tail), slice(0, below))):
                weights = jnp.exp2((score - top) * (SCALE * LOG2E)).astype(BF16)
                acc = acc + nn(weights, values[rows, :])
            ctx[:, aligned(j, HEAD)] = (acc[:, :HEAD] / acc[:, HEAD:]).astype(BF16)

        def some_heads(i, carry):
            scores = [head_scores(4 * i + e) for e in range(4)]
            for e in range(4):
                head_context(4 * i + e, scores[e])
            return carry

        lax.fori_loop(0, HEADS // 4, some_heads, 0)

    for chips in range(2, CHIPS + 1, 2):
        pl.when(chip // 2 == chips // 2 - 1)(lambda chips=chips: branch(chips))

    tops, totals, accs = [], [], []
    for k in range(CHIPS):
        stats = kvs[k][span:, HEAD:].astype(F32)
        tops.append(stats[:, 0:1] + stats[:, 16:17] + stats[:, 32:33])
        totals.append(stats[:, 48:49] + stats[:, 64:65] + stats[:, 80:81])
        accs.append(kvs[k][span:, :HEAD].astype(F32))
    top = tops[0]
    for value in tops[1:]:
        top = jnp.maximum(top, value)
    total, acc = 0.0, 0.0
    for k in range(CHIPS):
        factor = jnp.exp(tops[k] - top)
        total = total + totals[k] * factor
        acc = acc + accs[k] * factor
    merged = acc / total
    row_ctx[...] = jnp.zeros((ROWS, HEADS * HEAD), F32)
    for j in range(HEADS):
        row_ctx[:LIVE, j * HEAD : (j + 1) * HEAD] = merged[j * LIVE : (j + 1) * LIVE]


def factor_body(ids, oth, ctx, row_ctx, down0, down1, own_out, oth_out):
    core = ids[CORE]
    parts = HEADS * HEAD // CHUNK
    rows = row_ctx[...].astype(BF16)

    def place(i):
        return i ^ (2 * core)

    def block(at, t):
        total = jnp.zeros((RANK, BLOCK), F32)
        for i in range(parts):
            total += nt(jnp.where(t == 1, down1[place(i), 0], down0[place(i), 0]), ctx[aligned(at, BLOCK), i * CHUNK : (i + 1) * CHUNK])
        return total.astype(BF16)

    row_terms = []
    for t in range(2):
        total = jnp.zeros((ROWS, RANK), F32)
        for i in range(parts):
            total += nt(rows[:, i * CHUNK : (i + 1) * CHUNK], (down0, down1)[t][place(i), 0])
        row_terms.append(total)
    row_part = jnp.where(row_mask(ids, ROWS, RANK), row_terms[1], row_terms[0]).astype(BF16)
    for out, at, t in ((own_out, core, ids[OWN]), (oth_out, 1 - core, oth[0])):
        out[:RANK, :] = block(at, t)
        out[RANK:, :] = jnp.zeros((ROWS, BLOCK), BF16)
        out[RANK:, :RANK] = row_part


def out_body(ids, a, b, up, own_up, out, row_out):
    total = a[...].astype(F32) + b[...].astype(F32)
    factor = jnp.transpose(total[:RANK]).astype(BF16)
    for i in range(2 * CHIPS):
        out[:, i * CHUNK : (i + 1) * CHUNK] = nn(factor, up[SNAKE.index(i), 0]).astype(BF16)
    rows = total[RANK:, :RANK].astype(BF16)
    terms = [nn(rows, own_up[t]) for t in range(2)]
    row_out[...] = jnp.where(row_mask(ids, ROWS, CHUNK), terms[1], terms[0])[:LIVE].astype(BF16)


def per_device(
    prompt_hidden,
    prompt_qkv,
    block_tenant,
    row_hidden,
    row_qkv,
    row_tenant,
    row_cache,
    row_lengths,
    qkv_down,
    qkv_up,
    out_down,
    out_up,
):
    blk = lax.axis_index("blk")
    role = lax.axis_index("role")
    chip, core = blk // 2, blk % 2
    head = 2 * role + core
    ids = jnp.concatenate(
        [
            jnp.stack([role, chip, core]).astype(jnp.int32),
            block_tenant,
            row_tenant,
            row_lengths,
            jnp.stack([head, 2 * role + 1 - core]).astype(jnp.int32),
        ]
    )

    def to_core(value):
        return lax.ppermute(value, "blk", [(i, i ^ 1) for i in range(2 * CHIPS)])

    def to_role(value):
        return lax.ppermute(value, "role", [(0, 1), (1, 0)])

    down = jnp.transpose(qkv_down, (0, 2, 1))
    def to_x(value):
        return lax.ppermute(value, "blk", [(i, i ^ 2) for i in range(2 * CHIPS)])

    def from_row(value, dy):
        pairs = [((i + 4 * dy) % (2 * CHIPS), i) for i in range(2 * CHIPS)]
        return lax.ppermute(value, "blk", pairs)

    place = jnp.reshape(blk, (1,))
    (weights,) = call(
        pack_body,
        [place],
        [qkv_up, jnp.transpose(out_down, (0, 2, 1)), out_up],
        [None] * 3,
        [shape((7, RANK, CHUNK))],
        limit=48,
    )
    weights = lax.all_gather(weights, "blk", axis_index_groups=[SNAKE])
    arrived = from_row(down, 1)
    downs = [down, arrived, from_row(down, 3), from_row(down, 2)]
    hid, core_hid, x_hid, cross_hid = call(
        hidden_body,
        [place, block_tenant],
        [prompt_hidden],
        [pl.BlockSpec(memory_space=pl.ANY)],
        [shape((BLOCK + ROWS, 4 * CHUNK))] * 4,
        [pltpu.VMEM((ROWS, 4 * CHUNK), BF16), pltpu.SemaphoreType.DMA((20,))],
        48,
        out_specs=[pl.BlockSpec(memory_space=pl.ANY)] * 4,
    )
    cross_hid = lax.ppermute(cross_hid, "blk", [(i, i ^ 3) for i in range(2 * CHIPS)])
    x_hid, core_hid = to_x(x_hid), to_core(core_hid)
    base, base_send = call(
        base_body,
        [lax.optimization_barrier((ids, arrived))[0]],
        [prompt_qkv, row_cache],
        [pl.BlockSpec(memory_space=pl.ANY)] * 2,
        [shape((BLOCK, PACKED))] * 2,
        [pltpu.SemaphoreType.DMA((2 * (3 + 2 * (LIVE - 1)),))],
        48,
        out_specs=[pl.BlockSpec(memory_space=pl.ANY)] * 2,
    )
    base_oth = to_core(base_send)
    oth = to_core(block_tenant)
    row_hid = jnp.pad(row_hidden, ((0, ROWS - LIVE), (0, 0)))
    row_base = jnp.pad(row_qkv, ((0, ROWS - LIVE), (0, 0)))

    part, part_x = call(
        low_body,
        [ids],
        [hid, core_hid, x_hid, cross_hid, row_hid, *downs],
        [None] * 9,
        [shape((LOW_ROWS, HEAD))] * 2,
    )
    mine = (part.astype(F32) + to_x(part_x).astype(F32)).astype(BF16)
    mine = (mine.astype(F32) + to_core(mine).astype(F32)).astype(BF16)
    theirs = to_role(mine)
    row_columns = [
        spec((ROWS, HEADS * HEAD), lambda s: (0, s[HEAD_ID])),
        spec((ROWS, HEAD), lambda s: (0, 32 + s[HEAD_ID])),
        spec((ROWS, HEAD), lambda s: (0, 36 + s[HEAD_ID])),
    ]
    q, kv = call(
        proj_body,
        [ids, oth],
        [mine, theirs, base, base_oth] + [row_base] * 3 + [weights] * 3,
        [None] * 4
        + row_columns
        + [spec((2 * CHIPS, 1, RANK, CHUNK), lambda s, i=i: (0, i, 0, 0)) for i in range(3)],
        [shape((2 * BLOCK, HEADS * HEAD)), shape((2 * BLOCK + HEADS * LIVE, 2 * HEAD))],
        [pltpu.VMEM((CHIPS, 2, RANK, 5 * HEAD), BF16)],
        58,
    )
    kvs = gather_chips(kv)
    ctx, row_ctx = call(
        attend_body,
        [ids],
        [q, *kvs],
        [None] * (1 + CHIPS),
        [shape((2 * BLOCK, HEADS * HEAD)), shape((ROWS, HEADS * HEAD), F32)],
        [pltpu.VMEM((CHIPS * 2 * BLOCK, HEAD), BF16), pltpu.VMEM((CHIPS * 2 * BLOCK, 2 * HEAD), BF16)],
        32,
    )
    own, other = call(
        factor_body,
        [ids, oth],
        [ctx, row_ctx, weights, weights],
        [None, None]
        + [spec((4, 1, RANK, CHUNK), lambda s, t=t: (s[HEAD_ID], 3 + t, 0, 0)) for t in range(2)],
        [shape((RANK + ROWS, BLOCK)), shape((RANK + ROWS, BLOCK))],
        limit=48,
    )
    mine = (own.astype(F32) + to_core(other).astype(F32)).astype(BF16)
    return tuple(
        call(
            out_body,
            [ids],
            [mine, to_role(mine), weights, out_up],
            [None, None, spec((2 * CHIPS, 1, RANK, CHUNK), lambda s: (0, 5 + s[OWN], 0, 0)), None],
            [shape(prompt_hidden.shape), shape((LIVE, CHUNK))],
            limit=48,
        )
    )


def solution(mesh):
    in_specs = (
        P(("grp", "blk"), "role"),
        P(("grp", "blk"), None),
        P(("grp", "blk")),
        P("grp", None),
        P("grp", None),
        P("grp"),
        P("grp", "blk", None),
        P("grp"),
        P(None, ("role", "blk"), None),
        P(None, None, "blk"),
        P(None, "blk", None),
        P(None, None, ("role", "blk")),
    )
    out_specs = (P(("grp", "blk"), "role"), P("grp", ("role", "blk")))
    return jax.shard_map(
        per_device, mesh=mesh, in_specs=in_specs, out_specs=out_specs, check_vma=False
    )
```

```python
import jax
import jax.numpy as jnp
from jax import lax
from jax.experimental import pallas as pl
from jax.experimental.pallas import tpu as pltpu
from jax.sharding import PartitionSpec as P

HEADS = 8
HEAD = 128
RANK = 64
BLOCK = 128
CHIPS = 8
CHUNK = 256
ROWS = 16
LIVE = 4
SCALE = HEAD ** -0.5
LOG2E = 1.4426950408889634
NEG = -1e30
F32 = jnp.float32
BF16 = jnp.bfloat16
MIB = 1 << 20

ROLE, CHIP, CORE, OWN, ROW_T, LENGTH, HEAD_ID, HEAD_OTHER, SCALARS = 0, 1, 2, 3, 4, 8, 11, 12, 13


def nt(a, b):
    return lax.dot_general(a, b, (((1,), (1,)), ((), ())), preferred_element_type=F32)


def nn(a, b):
    return jnp.dot(a, b, preferred_element_type=F32)


def aligned(index, size):
    return pl.ds(pl.multiple_of(index * size, size), size)


def call(body, scalars, args, in_specs, outs, scratch=(), limit=16, out_specs=None):
    def whole(shape):
        zeros = (0,) * len(shape)
        return pl.BlockSpec(shape, lambda i, *s: zeros)

    specs = [whole(a.shape) if spec is None else spec for a, spec in zip(args, in_specs)]
    return pl.pallas_call(
        body,
        grid_spec=pltpu.PrefetchScalarGridSpec(
            num_scalar_prefetch=len(scalars),
            grid=(1,),
            in_specs=specs,
            out_specs=out_specs or [whole(o.shape) for o in outs],
            scratch_shapes=list(scratch),
        ),
        out_shape=outs,
        compiler_params=pltpu.CompilerParams(vmem_limit_bytes=limit * MIB),
    )(*scalars, *args)


def spec(shape, place):
    return pl.BlockSpec(shape, lambda i, ids, *s: place(ids))


def shape(dims, dtype=BF16):
    return jax.ShapeDtypeStruct(dims, dtype)


STEPS = ((0, 0), (0, 1), (1, 0), (3, 0), (1, 1), (3, 1), (2, 0), (2, 1))


def source(chip, step):
    dy, dx = step
    return lax.rem(chip // 2 + dy, 4) * 2 + (lax.rem(chip, 2) ^ dx)


def gather_chips(value):
    def get(value, step):
        pairs = []
        for i in range(2 * CHIPS):
            y, x, core = i // 4, i // 2 % 2, i % 2
            pairs.append(((y + step[0]) % 4 * 4 + (x ^ step[1]) * 2 + core, i))
        return lax.ppermute(value, "blk", pairs)

    up = get(value, (1, 0))
    down_across = get(value, (3, 1))
    across = get(value, (0, 1))
    down = get(value, (3, 0))
    up_across = get(value, (1, 1))
    far = get(up, (1, 0))
    far_across = get(down_across, (3, 0))
    return [value, across, up, down, up_across, down_across, far, far_across]


def pack_body(
    place, adapter, hid, up, down, out_up, own, to_core, to_x, to_cross, weights, hid_in, up_in, mixed, tenant, sems
):
    x, core = lax.rem(place[0] // 2, 2), lax.rem(place[0], 2)
    copies = []

    def move(src, dst):
        copies.append(pltpu.make_async_copy(src, dst, sems.at[len(copies)]))
        copies[-1].start()
        return copies[-1]

    reads = [
        move(hid, hid_in),
        move(up, up_in),
        move(down, mixed.at[3:5]),
        move(out_up, mixed.at[5:7]),
    ]
    tenant[...] = jnp.full((ROWS, 4 * CHUNK), adapter[0].astype(F32)).astype(BF16)
    reads[0].wait()
    writes = []
    for out, dx, dc in ((to_x, 1, 0), (to_cross, 1, 1), (to_core, 0, 1), (own, 0, 0)):
        for y in range(4):
            chunk = 4 * y + 2 * (x ^ dx) + (core ^ dc)
            writes.append(move(hid_in.at[:, aligned(chunk, CHUNK)], out.at[:BLOCK, y * CHUNK : (y + 1) * CHUNK]))
        writes.append(move(tenant, out.at[BLOCK:, :]))
    for read in reads[1:]:
        read.wait()

    def columns(main, tail, at):
        for t in range(2):
            mixed[t] = up_in[t, :, main : main + CHUNK]
            mixed[2, :, t * HEAD : (t + 1) * HEAD] = jnp.zeros((RANK, HEAD), BF16)
            mixed[2, :, t * HEAD + at : t * HEAD + at + RANK] = up_in[t, :, tail : tail + RANK]

    pl.when(core == 0)(lambda: columns(0, CHUNK, 0))
    pl.when(core == 1)(lambda: columns(RANK, 0, RANK))
    writes.append(move(mixed, weights))
    for write in writes:
        write.wait()


CACHE_AT = (HEADS + 2) * HEAD
PACKED = CACHE_AT + (LIVE - 1) * 2 * HEAD


def base_body(ids, qkv, cache, own, other, sems):
    copies = []

    def move(src, out, at, width):
        copies.append(pltpu.make_async_copy(src, out.at[:, at : at + width], sems.at[len(copies)]))

    for out, head in ((own, ids[HEAD_ID]), (other, ids[HEAD_OTHER])):
        move(qkv.at[:, aligned(head, HEADS * HEAD)], out, 0, HEADS * HEAD)
        move(qkv.at[:, aligned(32 + head, HEAD)], out, HEADS * HEAD, HEAD)
        move(qkv.at[:, aligned(36 + head, HEAD)], out, (HEADS + 1) * HEAD, HEAD)
        for r in range(LIVE - 1):
            for half in range(2):
                at = CACHE_AT + (2 * r + half) * HEAD
                move(cache.at[r, :, aligned(4 * half + head, HEAD)], out, at, HEAD)
    for copy in copies:
        copy.start()
    for copy in copies:
        copy.wait()


LOW_ROWS = 3 * BLOCK + 2 * ROWS


def low_body(ids, own, by_core, by_x, by_cross, row_hid, w0, w1, w3, w2, mine, theirs):
    role, y, x, core = ids[ROLE], ids[CHIP] // 2, lax.rem(ids[CHIP], 2), ids[CORE]
    sums = [[jnp.zeros((n, 3 * RANK), F32) for _ in range(2)] for n in (BLOCK, BLOCK, BLOCK, BLOCK, ROWS)]
    for dy, w in ((0, w0), (1, w1), (3, w3), (2, w2)):
        src = lax.rem(y + dy, 4)
        parts = [hid[:BLOCK, aligned(src, CHUNK)] for hid in (own, by_core, by_x, by_cross)]
        parts.append(row_hid[:, aligned(role * 2 * CHIPS + 4 * src + 2 * x + core, CHUNK)])
        for total, part in zip(sums, parts):
            for t in range(2):
                total[t] += nt(part, w[t])

    def chosen(at, hid):
        adapter = jnp.broadcast_to(hid[BLOCK : BLOCK + 1, : 3 * RANK].astype(F32), (BLOCK, 3 * RANK))
        return jnp.where(adapter > 0.5, sums[at][1], sums[at][0])

    rows = jnp.where(row_mask(ids, ROWS, 3 * RANK), sums[4][1], sums[4][0]).astype(BF16)
    for out, (first, one), (second, two) in (
        (mine, (0, own), (1, by_core)),
        (theirs, (2, by_x), (3, by_cross)),
    ):
        first, second = chosen(first, one), chosen(second, two)
        even, odd = jnp.where(core == 0, first, second), jnp.where(core == 0, second, first)
        out[:BLOCK, :] = even[:, :HEAD].astype(BF16)
        out[BLOCK : 2 * BLOCK, :] = odd[:, :HEAD].astype(BF16)
        out[2 * BLOCK : 3 * BLOCK, :] = jnp.concatenate([even[:, HEAD:], odd[:, HEAD:]], axis=1).astype(BF16)
        out[3 * BLOCK : 3 * BLOCK + ROWS, :] = rows[:, :HEAD]
        out[3 * BLOCK + ROWS :, :RANK] = rows[:, HEAD:]
        out[3 * BLOCK + ROWS :, RANK:] = jnp.zeros((ROWS, RANK), BF16)


def row_mask(ids, rows, width):
    at = lax.broadcasted_iota(jnp.int32, (rows, width), 0)
    mask = jnp.zeros((rows, width), jnp.int32)
    for r in range(LIVE):
        mask = jnp.where(at == r, ids[ROW_T + r], mask)
    return mask == 1


def split3(x):
    hi = x.astype(BF16).astype(F32)
    mid = (x - hi).astype(BF16).astype(F32)
    return hi, mid, x - hi - mid


def cached(r, half):
    at = CACHE_AT + (2 * r + half) * HEAD
    return slice(at, at + HEAD)


def proj_body(
    ids, oth, mine, theirs, base, base_oth, rq, rk, rv, up0, up1, tail, q_out, kv_out, upb
):
    chip, core, head = ids[CHIP], ids[CORE], ids[HEAD_ID]
    for src in range(CHIPS):
        for t, up in enumerate((up0, up1)):
            lanes = slice(t * HEAD, (t + 1) * HEAD)
            upb[src, t, :, : 2 * HEAD] = up[2 * src, 0]
            upb[src, t, :, 2 * HEAD : 3 * HEAD] = tail[2 * src, 0, :, lanes] + tail[2 * src + 1, 0, :, lanes]
            upb[src, t, :, 3 * HEAD :] = up[2 * src + 1, 0]
    own_rows, oth_rows = aligned(core, BLOCK), aligned(1 - core, BLOCK)

    def low(rows):
        return (mine[rows, :].astype(F32) + theirs[rows, :].astype(F32)).astype(BF16)

    third = low(slice(2 * BLOCK, 3 * BLOCK))
    thirds = third[:, :RANK], third[:, RANK:]
    low_own = jnp.concatenate([low(own_rows), jnp.where(core == 0, *thirds)], axis=1)
    low_oth = jnp.concatenate([low(oth_rows), jnp.where(core == 1, *thirds)], axis=1)
    low_row = jnp.concatenate(
        [low(slice(3 * BLOCK, 3 * BLOCK + ROWS)), low(slice(3 * BLOCK + ROWS, LOW_ROWS))[:, :RANK]], axis=1
    )
    mask = row_mask(ids, ROWS, HEAD)
    row_q = []
    new_k = new_v = k_own = k_oth = v_own = v_oth = None
    for j in range(HEADS + 2):
        group = max(j - HEADS + 1, 0)
        tile = head * HEADS + j if j < HEADS else head + (32 if j == HEADS else 36)
        src, off = lax.div(tile, 5), lax.rem(tile, 5)
        columns = aligned(off, HEAD)
        part = slice(group * RANK, (group + 1) * RANK)
        here = slice(j * HEAD, (j + 1) * HEAD)
        row_base = (rq[:, here] if j < HEADS else (rk if j == HEADS else rv)[...]).astype(F32)
        got_own = (base[:, here].astype(F32) + nn(low_own[:, part], upb[src, ids[OWN], :, columns])).astype(BF16)
        got_oth = (base_oth[:, here].astype(F32) + nn(low_oth[:, part], upb[src, oth[0], :, columns])).astype(BF16)
        row_terms = [nn(low_row[:, part], upb[src, t, :, columns]) for t in range(2)]
        got_row = (row_base + jnp.where(mask, row_terms[1], row_terms[0])).astype(BF16)
        if j < HEADS:
            q_out[own_rows, here] = got_own
            q_out[oth_rows, here] = got_oth
            row_q.append(got_row)
        elif j == HEADS:
            kv_out[own_rows, :HEAD] = got_own
            kv_out[oth_rows, :HEAD] = got_oth
            k_own, k_oth, new_k = got_own, got_oth, got_row
        else:
            kv_out[own_rows, HEAD:] = got_own
            kv_out[oth_rows, HEAD:] = got_oth
            v_own, v_oth, new_v = got_own, got_oth, got_row

    count = HEADS * ROWS
    queries = jnp.concatenate(row_q, axis=0)
    row_id = lax.rem(lax.broadcasted_iota(jnp.int32, (count, BLOCK), 0), ROWS)
    lane = lax.broadcasted_iota(jnp.int32, (count, BLOCK), 1)
    halves = []
    for at, first in ((core, 0), (1 - core, 1)):
        scores = nt(queries, k_oth if first else k_own)
        valid = jnp.full((count, BLOCK), 1, jnp.int32)
        position = (2 * chip + at) * BLOCK + lane
        for r in range(LIVE - 1):
            keys = (base_oth if first else base)[:, cached(r, 0)]
            this = row_id == r + 1
            scores = jnp.where(this, nt(queries, keys), scores)
            valid = jnp.where(this, (position < ids[LENGTH + r]).astype(jnp.int32), valid)
        halves.append((jnp.where(valid == 1, scores * SCALE, NEG), valid == 1))
    own_lane = lax.broadcasted_iota(jnp.int32, (count, ROWS), 1)
    own_row = lax.rem(lax.broadcasted_iota(jnp.int32, (count, ROWS), 0), ROWS)
    first_chip = chip == 0
    own_score = jnp.where((own_lane == own_row) & first_chip, nt(queries, new_k) * SCALE, NEG)
    top = jnp.max(jnp.maximum(halves[0][0], halves[1][0]), axis=1, keepdims=True)
    top = jnp.maximum(top, jnp.max(own_score, axis=1, keepdims=True))
    own_weight = jnp.where((own_lane == own_row) & first_chip, jnp.exp(own_score - top), 0.0)
    total = jnp.sum(own_weight, axis=1, keepdims=True)
    acc = nn(own_weight.astype(BF16), new_v)
    for first, (scores, valid) in enumerate(halves):
        weights = jnp.where(valid, jnp.exp(scores - top), 0.0)
        total = total + jnp.sum(weights, axis=1, keepdims=True)
        for r in range(LIVE):
            if r == 0:
                values = v_oth if first else v_own
            else:
                values = (base_oth if first else base)[:, cached(r - 1, 1)]
            acc = acc + nn(jnp.where(row_id == r, weights, 0.0).astype(BF16), values)
    stats = jnp.zeros((count, HEAD), F32)
    for place, value in enumerate(split3(top) + split3(total)):
        stats = jnp.where(lane // 16 == place, value, stats)
    keep_row = lax.broadcasted_iota(jnp.int32, (HEADS * LIVE, count), 0)
    keep_from = lax.broadcasted_iota(jnp.int32, (HEADS * LIVE, count), 1)
    keep = jnp.where((keep_row // LIVE) * ROWS + keep_row % LIVE == keep_from, 1.0, 0.0).astype(BF16)
    kv_out[2 * BLOCK :, :HEAD] = nn(keep, acc.astype(BF16)).astype(BF16)
    kv_out[2 * BLOCK :, HEAD:] = nn(keep, stats.astype(BF16)).astype(BF16)


def attend_body(ids, q, *rest):
    kvs, (ctx, row_ctx), (keys, values) = rest[:CHIPS], rest[CHIPS : CHIPS + 2], rest[CHIPS + 2 :]
    chip = ids[CHIP]
    span = 2 * BLOCK
    values[:, HEAD:] = jnp.ones((CHIPS * span, HEAD), BF16)
    for k in range(CHIPS):
        keys[aligned(source(chip, STEPS[k]), span), :] = kvs[k][:span, :HEAD]
        values[aligned(source(chip, STEPS[k]), span), :HEAD] = kvs[k][:span, HEAD:]

    def branch(chips):
        below, tail = (chips - 2) * span, 2 * span

        def head_scores(j):
            queries = q[:, aligned(j, HEAD)]
            last = nt(queries, keys[below : below + tail, :])
            row = lax.broadcasted_iota(jnp.int32, (span, tail), 0) + (chip - (chips - 2)) * span
            col = lax.broadcasted_iota(jnp.int32, (span, tail), 1)
            scores = [jnp.where(col <= row, last, NEG)]
            if below:
                scores.append(nt(queries, keys[:below, :]))
            return scores

        def head_context(j, scores):
            top = jnp.max(scores[0], axis=1, keepdims=True)
            if below:
                top = jnp.maximum(top, jnp.max(scores[1], axis=1, keepdims=True))
            acc = 0.0
            for score, rows in zip(scores, (slice(below, below + tail), slice(0, below))):
                weights = jnp.exp2((score - top) * (SCALE * LOG2E)).astype(BF16)
                acc = acc + nn(weights, values[rows, :])
            ctx[:, aligned(j, HEAD)] = (acc[:, :HEAD] / acc[:, HEAD:]).astype(BF16)

        def some_heads(i, carry):
            scores = [head_scores(4 * i + e) for e in range(4)]
            for e in range(4):
                head_context(4 * i + e, scores[e])
            return carry

        lax.fori_loop(0, HEADS // 4, some_heads, 0)

    for chips in range(2, CHIPS + 1, 2):
        pl.when(chip // 2 == chips // 2 - 1)(lambda chips=chips: branch(chips))

    tops, totals, accs = [], [], []
    for k in range(CHIPS):
        stats = kvs[k][span:, HEAD:].astype(F32)
        tops.append(stats[:, 0:1] + stats[:, 16:17] + stats[:, 32:33])
        totals.append(stats[:, 48:49] + stats[:, 64:65] + stats[:, 80:81])
        accs.append(kvs[k][span:, :HEAD].astype(F32))
    top = tops[0]
    for value in tops[1:]:
        top = jnp.maximum(top, value)
    total, acc = 0.0, 0.0
    for k in range(CHIPS):
        factor = jnp.exp(tops[k] - top)
        total = total + totals[k] * factor
        acc = acc + accs[k] * factor
    merged = acc / total
    row_ctx[...] = jnp.zeros((ROWS, HEADS * HEAD), F32)
    for j in range(HEADS):
        row_ctx[:LIVE, j * HEAD : (j + 1) * HEAD] = merged[j * LIVE : (j + 1) * LIVE]


def factor_body(ids, oth, ctx, row_ctx, down0, down1, own_out, oth_out):
    core = ids[CORE]
    parts = HEADS * HEAD // CHUNK
    rows = row_ctx[...].astype(BF16)

    def block(at, t):
        total = jnp.zeros((RANK, BLOCK), F32)
        for i in range(parts):
            total += nt(jnp.where(t == 1, down1[i, 0], down0[i, 0]), ctx[aligned(at, BLOCK), i * CHUNK : (i + 1) * CHUNK])
        return total.astype(BF16)

    row_terms = []
    for t in range(2):
        total = jnp.zeros((ROWS, RANK), F32)
        for i in range(parts):
            total += nt(rows[:, i * CHUNK : (i + 1) * CHUNK], (down0, down1)[t][i, 0])
        row_terms.append(total)
    row_part = jnp.where(row_mask(ids, ROWS, RANK), row_terms[1], row_terms[0]).astype(BF16)
    for out, at, t in ((own_out, core, ids[OWN]), (oth_out, 1 - core, oth[0])):
        out[:RANK, :] = block(at, t)
        out[RANK:, :] = jnp.zeros((ROWS, BLOCK), BF16)
        out[RANK:, :RANK] = row_part


def out_body(ids, a, b, up, own_up, out, row_out):
    total = a[...].astype(F32) + b[...].astype(F32)
    factor = jnp.transpose(total[:RANK]).astype(BF16)
    for i in range(2 * CHIPS):
        out[:, i * CHUNK : (i + 1) * CHUNK] = nn(factor, up[i, 0]).astype(BF16)
    rows = total[RANK:, :RANK].astype(BF16)
    terms = [nn(rows, own_up[t]) for t in range(2)]
    row_out[...] = jnp.where(row_mask(ids, ROWS, CHUNK), terms[1], terms[0])[:LIVE].astype(BF16)


def per_device(
    prompt_hidden,
    prompt_qkv,
    block_tenant,
    row_hidden,
    row_qkv,
    row_tenant,
    row_cache,
    row_lengths,
    qkv_down,
    qkv_up,
    out_down,
    out_up,
):
    blk = lax.axis_index("blk")
    role = lax.axis_index("role")
    chip, core = blk // 2, blk % 2
    head = 2 * role + core
    ids = jnp.concatenate(
        [
            jnp.stack([role, chip, core]).astype(jnp.int32),
            block_tenant,
            row_tenant,
            row_lengths,
            jnp.stack([head, 2 * role + 1 - core]).astype(jnp.int32),
        ]
    )

    def to_core(value):
        return lax.ppermute(value, "blk", [(i, i ^ 1) for i in range(2 * CHIPS)])

    def to_role(value):
        return lax.ppermute(value, "role", [(0, 1), (1, 0)])

    down = jnp.transpose(qkv_down, (0, 2, 1))
    def to_x(value):
        return lax.ppermute(value, "blk", [(i, i ^ 2) for i in range(2 * CHIPS)])

    def from_row(value, dy):
        pairs = [((i + 4 * dy) % (2 * CHIPS), i) for i in range(2 * CHIPS)]
        return lax.ppermute(value, "blk", pairs)

    place = jnp.reshape(blk, (1,))
    hid, core_hid, x_hid, cross_hid, weights = call(
        pack_body,
        [place, block_tenant],
        [prompt_hidden, qkv_up, jnp.transpose(out_down, (0, 2, 1)), out_up],
        [pl.BlockSpec(memory_space=pltpu.HBM)] * 4,
        [shape((BLOCK + ROWS, 4 * CHUNK))] * 4 + [shape((7, RANK, CHUNK))],
        [
            pltpu.VMEM(prompt_hidden.shape, BF16),
            pltpu.VMEM(qkv_up.shape, BF16),
            pltpu.VMEM((7, RANK, CHUNK), BF16),
            pltpu.VMEM((ROWS, 4 * CHUNK), BF16),
            pltpu.SemaphoreType.DMA((25,)),
        ],
        63,
        out_specs=[pl.BlockSpec(memory_space=pl.ANY)] * 5,
    )
    weights = lax.all_gather(weights, "blk")
    cross_hid = lax.ppermute(cross_hid, "blk", [(i, i ^ 3) for i in range(2 * CHIPS)])
    x_hid, core_hid = to_x(x_hid), to_core(core_hid)
    downs = [down, from_row(down, 1), from_row(down, 3), from_row(down, 2)]
    base, base_send = call(
        base_body,
        [lax.optimization_barrier((ids, x_hid))[0]],
        [prompt_qkv, row_cache],
        [pl.BlockSpec(memory_space=pltpu.HBM)] * 2,
        [shape((BLOCK, PACKED))] * 2,
        [pltpu.SemaphoreType.DMA((2 * (3 + 2 * (LIVE - 1)),))],
        out_specs=[pl.BlockSpec(memory_space=pl.ANY)] * 2,
    )
    base_oth = to_core(base_send)
    oth = to_core(block_tenant)
    row_hid = jnp.pad(row_hidden, ((0, ROWS - LIVE), (0, 0)))
    row_base = jnp.pad(row_qkv, ((0, ROWS - LIVE), (0, 0)))

    part, part_x = call(
        low_body,
        [ids],
        [hid, core_hid, x_hid, cross_hid, row_hid, *downs],
        [None] * 9,
        [shape((LOW_ROWS, HEAD))] * 2,
    )
    mine = (part.astype(F32) + to_x(part_x).astype(F32)).astype(BF16)
    mine = (mine.astype(F32) + to_core(mine).astype(F32)).astype(BF16)
    theirs = to_role(mine)
    row_columns = [
        spec((ROWS, HEADS * HEAD), lambda s: (0, s[HEAD_ID])),
        spec((ROWS, HEAD), lambda s: (0, 32 + s[HEAD_ID])),
        spec((ROWS, HEAD), lambda s: (0, 36 + s[HEAD_ID])),
    ]
    q, kv = call(
        proj_body,
        [ids, oth],
        [mine, theirs, base, base_oth] + [row_base] * 3 + [weights] * 3,
        [None] * 4
        + row_columns
        + [spec((2 * CHIPS, 1, RANK, CHUNK), lambda s, i=i: (0, i, 0, 0)) for i in range(3)],
        [shape((2 * BLOCK, HEADS * HEAD)), shape((2 * BLOCK + HEADS * LIVE, 2 * HEAD))],
        [pltpu.VMEM((CHIPS, 2, RANK, 5 * HEAD), BF16)],
        48,
    )
    kvs = gather_chips(kv)
    ctx, row_ctx = call(
        attend_body,
        [ids],
        [q, *kvs],
        [None] * (1 + CHIPS),
        [shape((2 * BLOCK, HEADS * HEAD)), shape((ROWS, HEADS * HEAD), F32)],
        [pltpu.VMEM((CHIPS * 2 * BLOCK, HEAD), BF16), pltpu.VMEM((CHIPS * 2 * BLOCK, 2 * HEAD), BF16)],
        32,
    )
    own, other = call(
        factor_body,
        [ids, oth],
        [ctx, row_ctx, weights, weights],
        [None, None]
        + [spec((4, 1, RANK, CHUNK), lambda s, t=t: (s[HEAD_ID], 3 + t, 0, 0)) for t in range(2)],
        [shape((RANK + ROWS, BLOCK)), shape((RANK + ROWS, BLOCK))],
        limit=48,
    )
    mine = (own.astype(F32) + to_core(other).astype(F32)).astype(BF16)
    return tuple(
        call(
            out_body,
            [ids],
            [mine, to_role(mine), weights, out_up],
            [None, None, spec((2 * CHIPS, 1, RANK, CHUNK), lambda s: (0, 5 + s[OWN], 0, 0)), None],
            [shape(prompt_hidden.shape), shape((LIVE, CHUNK))],
            limit=48,
        )
    )


def solution(mesh):
    in_specs = (
        P(("grp", "blk"), "role"),
        P(("grp", "blk"), None),
        P(("grp", "blk")),
        P("grp", None),
        P("grp", None),
        P("grp"),
        P("grp", "blk", None),
        P("grp"),
        P(None, ("role", "blk"), None),
        P(None, None, "blk"),
        P(None, "blk", None),
        P(None, None, ("role", "blk")),
    )
    out_specs = (P(("grp", "blk"), "role"), P("grp", ("role", "blk")))
    return jax.shard_map(
        per_device, mesh=mesh, in_specs=in_specs, out_specs=out_specs, check_vma=False
    )
```

```python
import jax
import jax.numpy as jnp
from jax import lax
from jax.experimental import pallas as pl
from jax.experimental.pallas import tpu as pltpu
from jax.sharding import PartitionSpec as P

HEADS = 8
HEAD = 128
RANK = 64
BLOCK = 128
CHIPS = 8
CHUNK = 256
ROWS = 16
LIVE = 4
SCALE = HEAD ** -0.5
LOG2E = 1.4426950408889634
NEG = -1e30
F32 = jnp.float32
BF16 = jnp.bfloat16
MIB = 1 << 20

ROLE, CHIP, CORE, OWN, ROW_T, LENGTH, HEAD_ID, HEAD_OTHER, SCALARS = 0, 1, 2, 3, 4, 8, 11, 12, 13


def nt(a, b):
    return lax.dot_general(a, b, (((1,), (1,)), ((), ())), preferred_element_type=F32)


def nn(a, b):
    return jnp.dot(a, b, preferred_element_type=F32)


def aligned(index, size):
    return pl.ds(pl.multiple_of(index * size, size), size)


def call(body, scalars, args, in_specs, outs, scratch=(), limit=16, out_specs=None):
    def whole(shape):
        zeros = (0,) * len(shape)
        return pl.BlockSpec(shape, lambda i, *s: zeros)

    specs = [whole(a.shape) if spec is None else spec for a, spec in zip(args, in_specs)]
    return pl.pallas_call(
        body,
        grid_spec=pltpu.PrefetchScalarGridSpec(
            num_scalar_prefetch=len(scalars),
            grid=(1,),
            in_specs=specs,
            out_specs=out_specs or [whole(o.shape) for o in outs],
            scratch_shapes=list(scratch),
        ),
        out_shape=outs,
        compiler_params=pltpu.CompilerParams(vmem_limit_bytes=limit * MIB),
    )(*scalars, *args)


def spec(shape, place):
    return pl.BlockSpec(shape, lambda i, ids, *s: place(ids))


def shape(dims, dtype=BF16):
    return jax.ShapeDtypeStruct(dims, dtype)


STEPS = ((0, 0), (0, 1), (1, 0), (3, 0), (1, 1), (3, 1), (2, 0), (2, 1))


def source(chip, step):
    dy, dx = step
    return lax.rem(chip // 2 + dy, 4) * 2 + (lax.rem(chip, 2) ^ dx)


def gather_chips(value):
    def get(value, step):
        pairs = []
        for i in range(2 * CHIPS):
            y, x, core = i // 4, i // 2 % 2, i % 2
            pairs.append(((y + step[0]) % 4 * 4 + (x ^ step[1]) * 2 + core, i))
        return lax.ppermute(value, "blk", pairs)

    up = get(value, (1, 0))
    down_across = get(value, (3, 1))
    across = get(value, (0, 1))
    down = get(value, (3, 0))
    up_across = get(value, (1, 1))
    far = get(up, (1, 0))
    far_across = get(down_across, (3, 0))
    return [value, across, up, down, up_across, down_across, far, far_across]


def pack_body(
    place, adapter, hid, up, down, out_up, own, to_core, to_x, to_cross, weights, hid_in, up_in, mixed, tenant, sems
):
    x, core = lax.rem(place[0] // 2, 2), lax.rem(place[0], 2)
    copies = []

    def move(src, dst):
        copies.append(pltpu.make_async_copy(src, dst, sems.at[len(copies)]))
        copies[-1].start()
        return copies[-1]

    reads = [
        move(hid, hid_in),
        move(up, up_in),
        move(down, mixed.at[3:5]),
        move(out_up, mixed.at[5:7]),
    ]
    tenant[...] = jnp.full((ROWS, 4 * CHUNK), adapter[0].astype(F32)).astype(BF16)
    reads[0].wait()
    writes = []
    for out, dx, dc in ((to_x, 1, 0), (to_cross, 1, 1), (to_core, 0, 1), (own, 0, 0)):
        for y in range(4):
            chunk = 4 * y + 2 * (x ^ dx) + (core ^ dc)
            writes.append(move(hid_in.at[:, aligned(chunk, CHUNK)], out.at[:BLOCK, y * CHUNK : (y + 1) * CHUNK]))
        writes.append(move(tenant, out.at[BLOCK:, :]))
    for read in reads[1:]:
        read.wait()

    def columns(main, tail, at):
        for t in range(2):
            mixed[t] = up_in[t, :, main : main + CHUNK]
            mixed[2, :, t * HEAD : (t + 1) * HEAD] = jnp.zeros((RANK, HEAD), BF16)
            mixed[2, :, t * HEAD + at : t * HEAD + at + RANK] = up_in[t, :, tail : tail + RANK]

    pl.when(core == 0)(lambda: columns(0, CHUNK, 0))
    pl.when(core == 1)(lambda: columns(RANK, 0, RANK))
    writes.append(move(mixed, weights))
    for write in writes:
        write.wait()


CACHE_AT = (HEADS + 2) * HEAD
PACKED = CACHE_AT + (LIVE - 1) * 2 * HEAD


def base_body(ids, qkv, cache, own, other, sems):
    copies = []

    def move(src, out, at, width):
        copies.append(pltpu.make_async_copy(src, out.at[:, at : at + width], sems.at[len(copies)]))

    for out, head in ((own, ids[HEAD_ID]), (other, ids[HEAD_OTHER])):
        move(qkv.at[:, aligned(head, HEADS * HEAD)], out, 0, HEADS * HEAD)
        move(qkv.at[:, aligned(32 + head, HEAD)], out, HEADS * HEAD, HEAD)
        move(qkv.at[:, aligned(36 + head, HEAD)], out, (HEADS + 1) * HEAD, HEAD)
        for r in range(LIVE - 1):
            for half in range(2):
                at = CACHE_AT + (2 * r + half) * HEAD
                move(cache.at[r, :, aligned(4 * half + head, HEAD)], out, at, HEAD)
    for copy in copies:
        copy.start()
    for copy in copies:
        copy.wait()


LOW_ROWS = 3 * BLOCK + 2 * ROWS


def low_body(ids, own, by_core, by_x, by_cross, row_hid, w0, w1, w3, w2, mine, theirs):
    role, y, x, core = ids[ROLE], ids[CHIP] // 2, lax.rem(ids[CHIP], 2), ids[CORE]
    sums = [[jnp.zeros((n, 3 * RANK), F32) for _ in range(2)] for n in (BLOCK, BLOCK, BLOCK, BLOCK, ROWS)]
    for dy, w in ((0, w0), (1, w1), (3, w3), (2, w2)):
        src = lax.rem(y + dy, 4)
        parts = [hid[:BLOCK, aligned(src, CHUNK)] for hid in (own, by_core, by_x, by_cross)]
        parts.append(row_hid[:, aligned(role * 2 * CHIPS + 4 * src + 2 * x + core, CHUNK)])
        for total, part in zip(sums, parts):
            for t in range(2):
                total[t] += nt(part, w[t])

    def chosen(at, hid):
        adapter = jnp.broadcast_to(hid[BLOCK : BLOCK + 1, : 3 * RANK].astype(F32), (BLOCK, 3 * RANK))
        return jnp.where(adapter > 0.5, sums[at][1], sums[at][0])

    rows = jnp.where(row_mask(ids, ROWS, 3 * RANK), sums[4][1], sums[4][0]).astype(BF16)
    for out, (first, one), (second, two) in (
        (mine, (0, own), (1, by_core)),
        (theirs, (2, by_x), (3, by_cross)),
    ):
        first, second = chosen(first, one), chosen(second, two)
        even, odd = jnp.where(core == 0, first, second), jnp.where(core == 0, second, first)
        out[:BLOCK, :] = even[:, :HEAD].astype(BF16)
        out[BLOCK : 2 * BLOCK, :] = odd[:, :HEAD].astype(BF16)
        out[2 * BLOCK : 3 * BLOCK, :] = jnp.concatenate([even[:, HEAD:], odd[:, HEAD:]], axis=1).astype(BF16)
        out[3 * BLOCK : 3 * BLOCK + ROWS, :] = rows[:, :HEAD]
        out[3 * BLOCK + ROWS :, :RANK] = rows[:, HEAD:]
        out[3 * BLOCK + ROWS :, RANK:] = jnp.zeros((ROWS, RANK), BF16)


def row_mask(ids, rows, width):
    at = lax.broadcasted_iota(jnp.int32, (rows, width), 0)
    mask = jnp.zeros((rows, width), jnp.int32)
    for r in range(LIVE):
        mask = jnp.where(at == r, ids[ROW_T + r], mask)
    return mask == 1


def split3(x):
    hi = x.astype(BF16).astype(F32)
    mid = (x - hi).astype(BF16).astype(F32)
    return hi, mid, x - hi - mid


def cached(r, half):
    at = CACHE_AT + (2 * r + half) * HEAD
    return slice(at, at + HEAD)


def proj_body(
    ids, oth, mine, theirs, base, base_oth, rq, rk, rv, up0, up1, tail, q_out, kv_out, upb
):
    chip, core, head = ids[CHIP], ids[CORE], ids[HEAD_ID]
    for src in range(CHIPS):
        for t, up in enumerate((up0, up1)):
            lanes = slice(t * HEAD, (t + 1) * HEAD)
            upb[src, t, :, : 2 * HEAD] = up[2 * src, 0]
            upb[src, t, :, 2 * HEAD : 3 * HEAD] = tail[2 * src, 0, :, lanes] + tail[2 * src + 1, 0, :, lanes]
            upb[src, t, :, 3 * HEAD :] = up[2 * src + 1, 0]
    own_rows, oth_rows = aligned(core, BLOCK), aligned(1 - core, BLOCK)

    def low(rows):
        return (mine[rows, :].astype(F32) + theirs[rows, :].astype(F32)).astype(BF16)

    third = low(slice(2 * BLOCK, 3 * BLOCK))
    thirds = third[:, :RANK], third[:, RANK:]
    low_own = jnp.concatenate([low(own_rows), jnp.where(core == 0, *thirds)], axis=1)
    low_oth = jnp.concatenate([low(oth_rows), jnp.where(core == 1, *thirds)], axis=1)
    low_row = jnp.concatenate(
        [low(slice(3 * BLOCK, 3 * BLOCK + ROWS)), low(slice(3 * BLOCK + ROWS, LOW_ROWS))[:, :RANK]], axis=1
    )
    mask = row_mask(ids, ROWS, HEAD)
    row_q = []
    new_k = new_v = k_own = k_oth = v_own = v_oth = None
    for j in range(HEADS + 2):
        group = max(j - HEADS + 1, 0)
        tile = head * HEADS + j if j < HEADS else head + (32 if j == HEADS else 36)
        src, off = lax.div(tile, 5), lax.rem(tile, 5)
        columns = aligned(off, HEAD)
        part = slice(group * RANK, (group + 1) * RANK)
        here = slice(j * HEAD, (j + 1) * HEAD)
        row_base = (rq[:, here] if j < HEADS else (rk if j == HEADS else rv)[...]).astype(F32)
        got_own = (base[:, here].astype(F32) + nn(low_own[:, part], upb[src, ids[OWN], :, columns])).astype(BF16)
        got_oth = (base_oth[:, here].astype(F32) + nn(low_oth[:, part], upb[src, oth[0], :, columns])).astype(BF16)
        row_terms = [nn(low_row[:, part], upb[src, t, :, columns]) for t in range(2)]
        got_row = (row_base + jnp.where(mask, row_terms[1], row_terms[0])).astype(BF16)
        if j < HEADS:
            q_out[own_rows, here] = got_own
            q_out[oth_rows, here] = got_oth
            row_q.append(got_row)
        elif j == HEADS:
            kv_out[own_rows, :HEAD] = got_own
            kv_out[oth_rows, :HEAD] = got_oth
            k_own, k_oth, new_k = got_own, got_oth, got_row
        else:
            kv_out[own_rows, HEAD:] = got_own
            kv_out[oth_rows, HEAD:] = got_oth
            v_own, v_oth, new_v = got_own, got_oth, got_row

    count = HEADS * ROWS
    queries = jnp.concatenate(row_q, axis=0)
    row_id = lax.rem(lax.broadcasted_iota(jnp.int32, (count, BLOCK), 0), ROWS)
    lane = lax.broadcasted_iota(jnp.int32, (count, BLOCK), 1)
    halves = []
    for at, first in ((core, 0), (1 - core, 1)):
        scores = nt(queries, k_oth if first else k_own)
        valid = jnp.full((count, BLOCK), 1, jnp.int32)
        position = (2 * chip + at) * BLOCK + lane
        for r in range(LIVE - 1):
            keys = (base_oth if first else base)[:, cached(r, 0)]
            this = row_id == r + 1
            scores = jnp.where(this, nt(queries, keys), scores)
            valid = jnp.where(this, (position < ids[LENGTH + r]).astype(jnp.int32), valid)
        halves.append((jnp.where(valid == 1, scores * SCALE, NEG), valid == 1))
    own_lane = lax.broadcasted_iota(jnp.int32, (count, ROWS), 1)
    own_row = lax.rem(lax.broadcasted_iota(jnp.int32, (count, ROWS), 0), ROWS)
    first_chip = chip == 0
    own_score = jnp.where((own_lane == own_row) & first_chip, nt(queries, new_k) * SCALE, NEG)
    top = jnp.max(jnp.maximum(halves[0][0], halves[1][0]), axis=1, keepdims=True)
    top = jnp.maximum(top, jnp.max(own_score, axis=1, keepdims=True))
    own_weight = jnp.where((own_lane == own_row) & first_chip, jnp.exp(own_score - top), 0.0)
    total = jnp.sum(own_weight, axis=1, keepdims=True)
    acc = nn(own_weight.astype(BF16), new_v)
    for first, (scores, valid) in enumerate(halves):
        weights = jnp.where(valid, jnp.exp(scores - top), 0.0)
        total = total + jnp.sum(weights, axis=1, keepdims=True)
        for r in range(LIVE):
            if r == 0:
                values = v_oth if first else v_own
            else:
                values = (base_oth if first else base)[:, cached(r - 1, 1)]
            acc = acc + nn(jnp.where(row_id == r, weights, 0.0).astype(BF16), values)
    stats = jnp.zeros((count, HEAD), F32)
    for place, value in enumerate(split3(top) + split3(total)):
        stats = jnp.where(lane // 16 == place, value, stats)
    keep_row = lax.broadcasted_iota(jnp.int32, (HEADS * LIVE, count), 0)
    keep_from = lax.broadcasted_iota(jnp.int32, (HEADS * LIVE, count), 1)
    keep = jnp.where((keep_row // LIVE) * ROWS + keep_row % LIVE == keep_from, 1.0, 0.0).astype(BF16)
    kv_out[2 * BLOCK :, :HEAD] = nn(keep, acc.astype(BF16)).astype(BF16)
    kv_out[2 * BLOCK :, HEAD:] = nn(keep, stats.astype(BF16)).astype(BF16)


def attend_body(ids, q, *rest):
    kvs, (ctx, row_ctx), (keys, values) = rest[:CHIPS], rest[CHIPS : CHIPS + 2], rest[CHIPS + 2 :]
    chip = ids[CHIP]
    span = 2 * BLOCK
    values[:, HEAD:] = jnp.ones((CHIPS * span, HEAD), BF16)
    for k in range(CHIPS):
        keys[aligned(source(chip, STEPS[k]), span), :] = kvs[k][:span, :HEAD]
        values[aligned(source(chip, STEPS[k]), span), :HEAD] = kvs[k][:span, HEAD:]

    def branch(chips):
        below, tail = (chips - 2) * span, 2 * span

        def head_scores(j):
            queries = q[:, aligned(j, HEAD)]
            last = nt(queries, keys[below : below + tail, :])
            row = lax.broadcasted_iota(jnp.int32, (span, tail), 0) + (chip - (chips - 2)) * span
            col = lax.broadcasted_iota(jnp.int32, (span, tail), 1)
            scores = [jnp.where(col <= row, last, NEG)]
            if below:
                scores.append(nt(queries, keys[:below, :]))
            return scores

        def head_context(j, scores):
            top = jnp.max(scores[0], axis=1, keepdims=True)
            if below:
                top = jnp.maximum(top, jnp.max(scores[1], axis=1, keepdims=True))
            acc = 0.0
            for score, rows in zip(scores, (slice(below, below + tail), slice(0, below))):
                weights = jnp.exp2((score - top) * (SCALE * LOG2E)).astype(BF16)
                acc = acc + nn(weights, values[rows, :])
            ctx[:, aligned(j, HEAD)] = (acc[:, :HEAD] / acc[:, HEAD:]).astype(BF16)

        def some_heads(i, carry):
            scores = [head_scores(4 * i + e) for e in range(4)]
            for e in range(4):
                head_context(4 * i + e, scores[e])
            return carry

        lax.fori_loop(0, HEADS // 4, some_heads, 0)

    for chips in range(2, CHIPS + 1, 2):
        pl.when(chip // 2 == chips // 2 - 1)(lambda chips=chips: branch(chips))

    tops, totals, accs = [], [], []
    for k in range(CHIPS):
        stats = kvs[k][span:, HEAD:].astype(F32)
        tops.append(stats[:, 0:1] + stats[:, 16:17] + stats[:, 32:33])
        totals.append(stats[:, 48:49] + stats[:, 64:65] + stats[:, 80:81])
        accs.append(kvs[k][span:, :HEAD].astype(F32))
    top = tops[0]
    for value in tops[1:]:
        top = jnp.maximum(top, value)
    total, acc = 0.0, 0.0
    for k in range(CHIPS):
        factor = jnp.exp(tops[k] - top)
        total = total + totals[k] * factor
        acc = acc + accs[k] * factor
    merged = acc / total
    row_ctx[...] = jnp.zeros((ROWS, HEADS * HEAD), F32)
    for j in range(HEADS):
        row_ctx[:LIVE, j * HEAD : (j + 1) * HEAD] = merged[j * LIVE : (j + 1) * LIVE]


def factor_body(ids, oth, ctx, row_ctx, down0, down1, own_out, oth_out):
    core = ids[CORE]
    parts = HEADS * HEAD // CHUNK
    rows = row_ctx[...].astype(BF16)

    def block(at, t):
        total = jnp.zeros((RANK, BLOCK), F32)
        for i in range(parts):
            total += nt(jnp.where(t == 1, down1[i, 0], down0[i, 0]), ctx[aligned(at, BLOCK), i * CHUNK : (i + 1) * CHUNK])
        return total.astype(BF16)

    row_terms = []
    for t in range(2):
        total = jnp.zeros((ROWS, RANK), F32)
        for i in range(parts):
            total += nt(rows[:, i * CHUNK : (i + 1) * CHUNK], (down0, down1)[t][i, 0])
        row_terms.append(total)
    row_part = jnp.where(row_mask(ids, ROWS, RANK), row_terms[1], row_terms[0]).astype(BF16)
    for out, at, t in ((own_out, core, ids[OWN]), (oth_out, 1 - core, oth[0])):
        out[:RANK, :] = block(at, t)
        out[RANK:, :] = jnp.zeros((ROWS, BLOCK), BF16)
        out[RANK:, :RANK] = row_part


def out_body(ids, a, b, up, own_up, out, row_out):
    total = a[...].astype(F32) + b[...].astype(F32)
    factor = jnp.transpose(total[:RANK]).astype(BF16)
    for i in range(2 * CHIPS):
        out[:, i * CHUNK : (i + 1) * CHUNK] = nn(factor, up[i, 0]).astype(BF16)
    rows = total[RANK:, :RANK].astype(BF16)
    terms = [nn(rows, own_up[t]) for t in range(2)]
    row_out[...] = jnp.where(row_mask(ids, ROWS, CHUNK), terms[1], terms[0])[:LIVE].astype(BF16)


def per_device(
    prompt_hidden,
    prompt_qkv,
    block_tenant,
    row_hidden,
    row_qkv,
    row_tenant,
    row_cache,
    row_lengths,
    qkv_down,
    qkv_up,
    out_down,
    out_up,
):
    blk = lax.axis_index("blk")
    role = lax.axis_index("role")
    chip, core = blk // 2, blk % 2
    head = 2 * role + core
    ids = jnp.concatenate(
        [
            jnp.stack([role, chip, core]).astype(jnp.int32),
            block_tenant,
            row_tenant,
            row_lengths,
            jnp.stack([head, 2 * role + 1 - core]).astype(jnp.int32),
        ]
    )

    def to_core(value):
        return lax.ppermute(value, "blk", [(i, i ^ 1) for i in range(2 * CHIPS)])

    def to_role(value):
        return lax.ppermute(value, "role", [(0, 1), (1, 0)])

    down = jnp.transpose(qkv_down, (0, 2, 1))
    def to_x(value):
        return lax.ppermute(value, "blk", [(i, i ^ 2) for i in range(2 * CHIPS)])

    def from_row(value, dy):
        pairs = [((i + 4 * dy) % (2 * CHIPS), i) for i in range(2 * CHIPS)]
        return lax.ppermute(value, "blk", pairs)

    place = jnp.reshape(blk, (1,))
    hid, core_hid, x_hid, cross_hid, weights = call(
        pack_body,
        [place, block_tenant],
        [prompt_hidden, qkv_up, jnp.transpose(out_down, (0, 2, 1)), out_up],
        [pl.BlockSpec(memory_space=pltpu.HBM)] * 4,
        [shape((BLOCK + ROWS, 4 * CHUNK))] * 4 + [shape((7, RANK, CHUNK))],
        [
            pltpu.VMEM(prompt_hidden.shape, BF16),
            pltpu.VMEM(qkv_up.shape, BF16),
            pltpu.VMEM((7, RANK, CHUNK), BF16),
            pltpu.VMEM((ROWS, 4 * CHUNK), BF16),
            pltpu.SemaphoreType.DMA((25,)),
        ],
        63,
        out_specs=[pl.BlockSpec(memory_space=pl.ANY)] * 5,
    )
    weights = lax.all_gather(weights, "blk")
    cross_hid = lax.ppermute(cross_hid, "blk", [(i, i ^ 3) for i in range(2 * CHIPS)])
    x_hid, core_hid = to_x(x_hid), to_core(core_hid)
    downs = [down, from_row(down, 1), from_row(down, 3), from_row(down, 2)]
    base, base_send = call(
        base_body,
        [lax.optimization_barrier((ids, x_hid))[0]],
        [prompt_qkv, row_cache],
        [pl.BlockSpec(memory_space=pltpu.HBM)] * 2,
        [shape((BLOCK, PACKED))] * 2,
        [pltpu.SemaphoreType.DMA((2 * (3 + 2 * (LIVE - 1)),))],
        out_specs=[pl.BlockSpec(memory_space=pl.ANY)] * 2,
    )
    base_oth = to_core(base_send)
    oth = to_core(block_tenant)
    row_hid = jnp.pad(row_hidden, ((0, ROWS - LIVE), (0, 0)))
    row_base = jnp.pad(row_qkv, ((0, ROWS - LIVE), (0, 0)))

    part, part_x = call(
        low_body,
        [ids],
        [hid, core_hid, x_hid, cross_hid, row_hid, *downs],
        [None] * 9,
        [shape((LOW_ROWS, HEAD))] * 2,
    )
    mine = (part.astype(F32) + to_x(part_x).astype(F32)).astype(BF16)
    mine = (mine.astype(F32) + to_core(mine).astype(F32)).astype(BF16)
    theirs = to_role(mine)
    row_columns = [
        spec((ROWS, HEADS * HEAD), lambda s: (0, s[HEAD_ID])),
        spec((ROWS, HEAD), lambda s: (0, 32 + s[HEAD_ID])),
        spec((ROWS, HEAD), lambda s: (0, 36 + s[HEAD_ID])),
    ]
    q, kv = call(
        proj_body,
        [ids, oth],
        [mine, theirs, base, base_oth] + [row_base] * 3 + [weights[:, :3]] * 3,
        [None] * 4
        + row_columns
        + [spec((2 * CHIPS, 1, RANK, CHUNK), lambda s, i=i: (0, i, 0, 0)) for i in range(3)],
        [shape((2 * BLOCK, HEADS * HEAD)), shape((2 * BLOCK + HEADS * LIVE, 2 * HEAD))],
        [pltpu.VMEM((CHIPS, 2, RANK, 5 * HEAD), BF16)],
        48,
    )
    kvs = gather_chips(kv)
    ctx, row_ctx = call(
        attend_body,
        [ids],
        [q, *kvs],
        [None] * (1 + CHIPS),
        [shape((2 * BLOCK, HEADS * HEAD)), shape((ROWS, HEADS * HEAD), F32)],
        [pltpu.VMEM((CHIPS * 2 * BLOCK, HEAD), BF16), pltpu.VMEM((CHIPS * 2 * BLOCK, 2 * HEAD), BF16)],
        32,
    )
    own, other = call(
        factor_body,
        [ids, oth],
        [ctx, row_ctx, weights, weights],
        [None, None]
        + [spec((4, 1, RANK, CHUNK), lambda s, t=t: (s[HEAD_ID], 3 + t, 0, 0)) for t in range(2)],
        [shape((RANK + ROWS, BLOCK)), shape((RANK + ROWS, BLOCK))],
        limit=48,
    )
    mine = (own.astype(F32) + to_core(other).astype(F32)).astype(BF16)
    return tuple(
        call(
            out_body,
            [ids],
            [mine, to_role(mine), weights, out_up],
            [None, None, spec((2 * CHIPS, 1, RANK, CHUNK), lambda s: (0, 5 + s[OWN], 0, 0)), None],
            [shape(prompt_hidden.shape), shape((LIVE, CHUNK))],
            limit=48,
        )
    )


def solution(mesh):
    in_specs = (
        P(("grp", "blk"), "role"),
        P(("grp", "blk"), None),
        P(("grp", "blk")),
        P("grp", None),
        P("grp", None),
        P("grp"),
        P("grp", "blk", None),
        P("grp"),
        P(None, ("role", "blk"), None),
        P(None, None, "blk"),
        P(None, "blk", None),
        P(None, None, ("role", "blk")),
    )
    out_specs = (P(("grp", "blk"), "role"), P("grp", ("role", "blk")))
    return jax.shard_map(
        per_device, mesh=mesh, in_specs=in_specs, out_specs=out_specs, check_vma=False
    )
```

```python
import jax
import jax.numpy as jnp
from jax import lax
from jax.experimental import pallas as pl
from jax.experimental.pallas import tpu as pltpu
from jax.sharding import PartitionSpec as P

HEADS = 8
HEAD = 128
RANK = 64
BLOCK = 128
CHIPS = 8
CHUNK = 256
ROWS = 16
LIVE = 4
SCALE = HEAD ** -0.5
LOG2E = 1.4426950408889634
NEG = -1e30
F32 = jnp.float32
BF16 = jnp.bfloat16
MIB = 1 << 20

ROLE, CHIP, CORE, OWN, ROW_T, LENGTH, HEAD_ID, HEAD_OTHER, SCALARS = 0, 1, 2, 3, 4, 8, 11, 12, 13


def nt(a, b):
    return lax.dot_general(a, b, (((1,), (1,)), ((), ())), preferred_element_type=F32)


def nn(a, b):
    return jnp.dot(a, b, preferred_element_type=F32)


def aligned(index, size):
    return pl.ds(pl.multiple_of(index * size, size), size)


def call(body, scalars, args, in_specs, outs, scratch=(), limit=16, out_specs=None):
    def whole(shape):
        zeros = (0,) * len(shape)
        return pl.BlockSpec(shape, lambda i, *s: zeros)

    specs = [whole(a.shape) if spec is None else spec for a, spec in zip(args, in_specs)]
    return pl.pallas_call(
        body,
        grid_spec=pltpu.PrefetchScalarGridSpec(
            num_scalar_prefetch=len(scalars),
            grid=(1,),
            in_specs=specs,
            out_specs=out_specs or [whole(o.shape) for o in outs],
            scratch_shapes=list(scratch),
        ),
        out_shape=outs,
        compiler_params=pltpu.CompilerParams(vmem_limit_bytes=limit * MIB),
    )(*scalars, *args)


def spec(shape, place):
    return pl.BlockSpec(shape, lambda i, ids, *s: place(ids))


def shape(dims, dtype=BF16):
    return jax.ShapeDtypeStruct(dims, dtype)


STEPS = ((0, 0), (0, 1), (1, 0), (3, 0), (1, 1), (3, 1), (2, 0), (2, 1))


def source(chip, step):
    dy, dx = step
    return lax.rem(chip // 2 + dy, 4) * 2 + (lax.rem(chip, 2) ^ dx)


def gather_chips(value):
    def get(value, step):
        pairs = []
        for i in range(2 * CHIPS):
            y, x, core = i // 4, i // 2 % 2, i % 2
            pairs.append(((y + step[0]) % 4 * 4 + (x ^ step[1]) * 2 + core, i))
        return lax.ppermute(value, "blk", pairs)

    up = get(value, (1, 0))
    down_across = get(value, (3, 1))
    across = get(value, (0, 1))
    down = get(value, (3, 0))
    up_across = get(value, (1, 1))
    far = get(up, (1, 0))
    far_across = get(down_across, (3, 0))
    return [value, across, up, down, up_across, down_across, far, far_across]


def pack_body(
    place, adapter, hid, up, down, out_up, own, to_core, to_x, to_cross, weights, hid_in, up_in, mixed, tenant, sems
):
    x, core = lax.rem(place[0] // 2, 2), lax.rem(place[0], 2)
    copies = []

    def move(src, dst):
        copies.append(pltpu.make_async_copy(src, dst, sems.at[len(copies)]))
        copies[-1].start()
        return copies[-1]

    reads = [
        move(up, up_in),
        move(down, mixed.at[3:5]),
        move(out_up, mixed.at[5:7]),
        move(hid, hid_in),
    ]
    tenant[...] = jnp.full((ROWS, 4 * CHUNK), adapter[0].astype(F32)).astype(BF16)
    for read in reads[:3]:
        read.wait()

    def columns(main, tail, at):
        for t in range(2):
            mixed[t] = up_in[t, :, main : main + CHUNK]
            mixed[2, :, t * HEAD : (t + 1) * HEAD] = jnp.zeros((RANK, HEAD), BF16)
            mixed[2, :, t * HEAD + at : t * HEAD + at + RANK] = up_in[t, :, tail : tail + RANK]

    pl.when(core == 0)(lambda: columns(0, CHUNK, 0))
    pl.when(core == 1)(lambda: columns(RANK, 0, RANK))
    writes = [move(mixed, weights)]
    reads[3].wait()
    for out, dx, dc in ((to_x, 1, 0), (to_cross, 1, 1), (to_core, 0, 1), (own, 0, 0)):
        for y in range(4):
            chunk = 4 * y + 2 * (x ^ dx) + (core ^ dc)
            writes.append(move(hid_in.at[:, aligned(chunk, CHUNK)], out.at[:BLOCK, y * CHUNK : (y + 1) * CHUNK]))
        writes.append(move(tenant, out.at[BLOCK:, :]))
    for write in writes:
        write.wait()


CACHE_AT = (HEADS + 2) * HEAD
PACKED = CACHE_AT + (LIVE - 1) * 2 * HEAD


def base_body(ids, qkv, cache, own, other, sems):
    copies = []

    def move(src, out, at, width):
        copies.append(pltpu.make_async_copy(src, out.at[:, at : at + width], sems.at[len(copies)]))

    for out, head in ((own, ids[HEAD_ID]), (other, ids[HEAD_OTHER])):
        move(qkv.at[:, aligned(head, HEADS * HEAD)], out, 0, HEADS * HEAD)
        move(qkv.at[:, aligned(32 + head, HEAD)], out, HEADS * HEAD, HEAD)
        move(qkv.at[:, aligned(36 + head, HEAD)], out, (HEADS + 1) * HEAD, HEAD)
        for r in range(LIVE - 1):
            for half in range(2):
                at = CACHE_AT + (2 * r + half) * HEAD
                move(cache.at[r, :, aligned(4 * half + head, HEAD)], out, at, HEAD)
    for copy in copies:
        copy.start()
    for copy in copies:
        copy.wait()


LOW_ROWS = 3 * BLOCK + 2 * ROWS


def low_body(ids, own, by_core, by_x, by_cross, row_hid, w0, w1, w3, w2, mine, theirs):
    role, y, x, core = ids[ROLE], ids[CHIP] // 2, lax.rem(ids[CHIP], 2), ids[CORE]
    sums = [[jnp.zeros((n, 3 * RANK), F32) for _ in range(2)] for n in (BLOCK, BLOCK, BLOCK, BLOCK, ROWS)]
    for dy, w in ((0, w0), (1, w1), (3, w3), (2, w2)):
        src = lax.rem(y + dy, 4)
        parts = [hid[:BLOCK, aligned(src, CHUNK)] for hid in (own, by_core, by_x, by_cross)]
        parts.append(row_hid[:, aligned(role * 2 * CHIPS + 4 * src + 2 * x + core, CHUNK)])
        for total, part in zip(sums, parts):
            for t in range(2):
                total[t] += nt(part, w[t])

    def chosen(at, hid):
        adapter = jnp.broadcast_to(hid[BLOCK : BLOCK + 1, : 3 * RANK].astype(F32), (BLOCK, 3 * RANK))
        return jnp.where(adapter > 0.5, sums[at][1], sums[at][0])

    rows = jnp.where(row_mask(ids, ROWS, 3 * RANK), sums[4][1], sums[4][0]).astype(BF16)
    for out, (first, one), (second, two) in (
        (mine, (0, own), (1, by_core)),
        (theirs, (2, by_x), (3, by_cross)),
    ):
        first, second = chosen(first, one), chosen(second, two)
        even, odd = jnp.where(core == 0, first, second), jnp.where(core == 0, second, first)
        out[:BLOCK, :] = even[:, :HEAD].astype(BF16)
        out[BLOCK : 2 * BLOCK, :] = odd[:, :HEAD].astype(BF16)
        out[2 * BLOCK : 3 * BLOCK, :] = jnp.concatenate([even[:, HEAD:], odd[:, HEAD:]], axis=1).astype(BF16)
        out[3 * BLOCK : 3 * BLOCK + ROWS, :] = rows[:, :HEAD]
        out[3 * BLOCK + ROWS :, :RANK] = rows[:, HEAD:]
        out[3 * BLOCK + ROWS :, RANK:] = jnp.zeros((ROWS, RANK), BF16)


def row_mask(ids, rows, width):
    at = lax.broadcasted_iota(jnp.int32, (rows, width), 0)
    mask = jnp.zeros((rows, width), jnp.int32)
    for r in range(LIVE):
        mask = jnp.where(at == r, ids[ROW_T + r], mask)
    return mask == 1


def split3(x):
    hi = x.astype(BF16).astype(F32)
    mid = (x - hi).astype(BF16).astype(F32)
    return hi, mid, x - hi - mid


def cached(r, half):
    at = CACHE_AT + (2 * r + half) * HEAD
    return slice(at, at + HEAD)


def proj_body(
    ids, oth, mine, theirs, base, base_oth, rq, rk, rv, up0, up1, tail, q_out, kv_out, upb
):
    chip, core, head = ids[CHIP], ids[CORE], ids[HEAD_ID]
    for src in range(CHIPS):
        for t, up in enumerate((up0, up1)):
            lanes = slice(t * HEAD, (t + 1) * HEAD)
            upb[src, t, :, : 2 * HEAD] = up[2 * src, 0]
            upb[src, t, :, 2 * HEAD : 3 * HEAD] = tail[2 * src, 0, :, lanes] + tail[2 * src + 1, 0, :, lanes]
            upb[src, t, :, 3 * HEAD :] = up[2 * src + 1, 0]
    own_rows, oth_rows = aligned(core, BLOCK), aligned(1 - core, BLOCK)

    def low(rows):
        return (mine[rows, :].astype(F32) + theirs[rows, :].astype(F32)).astype(BF16)

    third = low(slice(2 * BLOCK, 3 * BLOCK))
    thirds = third[:, :RANK], third[:, RANK:]
    low_own = jnp.concatenate([low(own_rows), jnp.where(core == 0, *thirds)], axis=1)
    low_oth = jnp.concatenate([low(oth_rows), jnp.where(core == 1, *thirds)], axis=1)
    low_row = jnp.concatenate(
        [low(slice(3 * BLOCK, 3 * BLOCK + ROWS)), low(slice(3 * BLOCK + ROWS, LOW_ROWS))[:, :RANK]], axis=1
    )
    mask = row_mask(ids, ROWS, HEAD)
    row_q = []
    new_k = new_v = k_own = k_oth = v_own = v_oth = None
    for j in range(HEADS + 2):
        group = max(j - HEADS + 1, 0)
        tile = head * HEADS + j if j < HEADS else head + (32 if j == HEADS else 36)
        src, off = lax.div(tile, 5), lax.rem(tile, 5)
        columns = aligned(off, HEAD)
        part = slice(group * RANK, (group + 1) * RANK)
        here = slice(j * HEAD, (j + 1) * HEAD)
        row_base = (rq[:, here] if j < HEADS else (rk if j == HEADS else rv)[...]).astype(F32)
        got_own = (base[:, here].astype(F32) + nn(low_own[:, part], upb[src, ids[OWN], :, columns])).astype(BF16)
        got_oth = (base_oth[:, here].astype(F32) + nn(low_oth[:, part], upb[src, oth[0], :, columns])).astype(BF16)
        row_terms = [nn(low_row[:, part], upb[src, t, :, columns]) for t in range(2)]
        got_row = (row_base + jnp.where(mask, row_terms[1], row_terms[0])).astype(BF16)
        if j < HEADS:
            q_out[own_rows, here] = got_own
            q_out[oth_rows, here] = got_oth
            row_q.append(got_row)
        elif j == HEADS:
            kv_out[own_rows, :HEAD] = got_own
            kv_out[oth_rows, :HEAD] = got_oth
            k_own, k_oth, new_k = got_own, got_oth, got_row
        else:
            kv_out[own_rows, HEAD:] = got_own
            kv_out[oth_rows, HEAD:] = got_oth
            v_own, v_oth, new_v = got_own, got_oth, got_row

    count = HEADS * ROWS
    queries = jnp.concatenate(row_q, axis=0)
    row_id = lax.rem(lax.broadcasted_iota(jnp.int32, (count, BLOCK), 0), ROWS)
    lane = lax.broadcasted_iota(jnp.int32, (count, BLOCK), 1)
    halves = []
    for at, first in ((core, 0), (1 - core, 1)):
        scores = nt(queries, k_oth if first else k_own)
        valid = jnp.full((count, BLOCK), 1, jnp.int32)
        position = (2 * chip + at) * BLOCK + lane
        for r in range(LIVE - 1):
            keys = (base_oth if first else base)[:, cached(r, 0)]
            this = row_id == r + 1
            scores = jnp.where(this, nt(queries, keys), scores)
            valid = jnp.where(this, (position < ids[LENGTH + r]).astype(jnp.int32), valid)
        halves.append((jnp.where(valid == 1, scores * SCALE, NEG), valid == 1))
    own_lane = lax.broadcasted_iota(jnp.int32, (count, ROWS), 1)
    own_row = lax.rem(lax.broadcasted_iota(jnp.int32, (count, ROWS), 0), ROWS)
    first_chip = chip == 0
    own_score = jnp.where((own_lane == own_row) & first_chip, nt(queries, new_k) * SCALE, NEG)
    top = jnp.max(jnp.maximum(halves[0][0], halves[1][0]), axis=1, keepdims=True)
    top = jnp.maximum(top, jnp.max(own_score, axis=1, keepdims=True))
    own_weight = jnp.where((own_lane == own_row) & first_chip, jnp.exp(own_score - top), 0.0)
    total = jnp.sum(own_weight, axis=1, keepdims=True)
    acc = nn(own_weight.astype(BF16), new_v)
    for first, (scores, valid) in enumerate(halves):
        weights = jnp.where(valid, jnp.exp(scores - top), 0.0)
        total = total + jnp.sum(weights, axis=1, keepdims=True)
        for r in range(LIVE):
            if r == 0:
                values = v_oth if first else v_own
            else:
                values = (base_oth if first else base)[:, cached(r - 1, 1)]
            acc = acc + nn(jnp.where(row_id == r, weights, 0.0).astype(BF16), values)
    stats = jnp.zeros((count, HEAD), F32)
    for place, value in enumerate(split3(top) + split3(total)):
        stats = jnp.where(lane // 16 == place, value, stats)
    keep_row = lax.broadcasted_iota(jnp.int32, (HEADS * LIVE, count), 0)
    keep_from = lax.broadcasted_iota(jnp.int32, (HEADS * LIVE, count), 1)
    keep = jnp.where((keep_row // LIVE) * ROWS + keep_row % LIVE == keep_from, 1.0, 0.0).astype(BF16)
    kv_out[2 * BLOCK :, :HEAD] = nn(keep, acc.astype(BF16)).astype(BF16)
    kv_out[2 * BLOCK :, HEAD:] = nn(keep, stats.astype(BF16)).astype(BF16)


def attend_body(ids, q, *rest):
    kvs, (ctx, row_ctx), (keys, values) = rest[:CHIPS], rest[CHIPS : CHIPS + 2], rest[CHIPS + 2 :]
    chip = ids[CHIP]
    span = 2 * BLOCK
    values[:, HEAD:] = jnp.ones((CHIPS * span, HEAD), BF16)
    for k in range(CHIPS):
        keys[aligned(source(chip, STEPS[k]), span), :] = kvs[k][:span, :HEAD]
        values[aligned(source(chip, STEPS[k]), span), :HEAD] = kvs[k][:span, HEAD:]

    def branch(chips):
        below, tail = (chips - 2) * span, 2 * span

        def head_scores(j):
            queries = q[:, aligned(j, HEAD)]
            last = nt(queries, keys[below : below + tail, :])
            row = lax.broadcasted_iota(jnp.int32, (span, tail), 0) + (chip - (chips - 2)) * span
            col = lax.broadcasted_iota(jnp.int32, (span, tail), 1)
            scores = [jnp.where(col <= row, last, NEG)]
            if below:
                scores.append(nt(queries, keys[:below, :]))
            return scores

        def head_context(j, scores):
            top = jnp.max(scores[0], axis=1, keepdims=True)
            if below:
                top = jnp.maximum(top, jnp.max(scores[1], axis=1, keepdims=True))
            acc = 0.0
            for score, rows in zip(scores, (slice(below, below + tail), slice(0, below))):
                weights = jnp.exp2((score - top) * (SCALE * LOG2E)).astype(BF16)
                acc = acc + nn(weights, values[rows, :])
            ctx[:, aligned(j, HEAD)] = (acc[:, :HEAD] / acc[:, HEAD:]).astype(BF16)

        def some_heads(i, carry):
            scores = [head_scores(4 * i + e) for e in range(4)]
            for e in range(4):
                head_context(4 * i + e, scores[e])
            return carry

        lax.fori_loop(0, HEADS // 4, some_heads, 0)

    for chips in range(2, CHIPS + 1, 2):
        pl.when(chip // 2 == chips // 2 - 1)(lambda chips=chips: branch(chips))

    tops, totals, accs = [], [], []
    for k in range(CHIPS):
        stats = kvs[k][span:, HEAD:].astype(F32)
        tops.append(stats[:, 0:1] + stats[:, 16:17] + stats[:, 32:33])
        totals.append(stats[:, 48:49] + stats[:, 64:65] + stats[:, 80:81])
        accs.append(kvs[k][span:, :HEAD].astype(F32))
    top = tops[0]
    for value in tops[1:]:
        top = jnp.maximum(top, value)
    total, acc = 0.0, 0.0
    for k in range(CHIPS):
        factor = jnp.exp(tops[k] - top)
        total = total + totals[k] * factor
        acc = acc + accs[k] * factor
    merged = acc / total
    row_ctx[...] = jnp.zeros((ROWS, HEADS * HEAD), F32)
    for j in range(HEADS):
        row_ctx[:LIVE, j * HEAD : (j + 1) * HEAD] = merged[j * LIVE : (j + 1) * LIVE]


def factor_body(ids, oth, ctx, row_ctx, down0, down1, own_out, oth_out):
    core = ids[CORE]
    parts = HEADS * HEAD // CHUNK
    rows = row_ctx[...].astype(BF16)

    def block(at, t):
        total = jnp.zeros((RANK, BLOCK), F32)
        for i in range(parts):
            total += nt(jnp.where(t == 1, down1[i, 0], down0[i, 0]), ctx[aligned(at, BLOCK), i * CHUNK : (i + 1) * CHUNK])
        return total.astype(BF16)

    row_terms = []
    for t in range(2):
        total = jnp.zeros((ROWS, RANK), F32)
        for i in range(parts):
            total += nt(rows[:, i * CHUNK : (i + 1) * CHUNK], (down0, down1)[t][i, 0])
        row_terms.append(total)
    row_part = jnp.where(row_mask(ids, ROWS, RANK), row_terms[1], row_terms[0]).astype(BF16)
    for out, at, t in ((own_out, core, ids[OWN]), (oth_out, 1 - core, oth[0])):
        out[:RANK, :] = block(at, t)
        out[RANK:, :] = jnp.zeros((ROWS, BLOCK), BF16)
        out[RANK:, :RANK] = row_part


def out_body(ids, a, b, up, own_up, out, row_out):
    total = a[...].astype(F32) + b[...].astype(F32)
    factor = jnp.transpose(total[:RANK]).astype(BF16)
    for i in range(2 * CHIPS):
        out[:, i * CHUNK : (i + 1) * CHUNK] = nn(factor, up[i, 0]).astype(BF16)
    rows = total[RANK:, :RANK].astype(BF16)
    terms = [nn(rows, own_up[t]) for t in range(2)]
    row_out[...] = jnp.where(row_mask(ids, ROWS, CHUNK), terms[1], terms[0])[:LIVE].astype(BF16)


def per_device(
    prompt_hidden,
    prompt_qkv,
    block_tenant,
    row_hidden,
    row_qkv,
    row_tenant,
    row_cache,
    row_lengths,
    qkv_down,
    qkv_up,
    out_down,
    out_up,
):
    blk = lax.axis_index("blk")
    role = lax.axis_index("role")
    chip, core = blk // 2, blk % 2
    head = 2 * role + core
    ids = jnp.concatenate(
        [
            jnp.stack([role, chip, core]).astype(jnp.int32),
            block_tenant,
            row_tenant,
            row_lengths,
            jnp.stack([head, 2 * role + 1 - core]).astype(jnp.int32),
        ]
    )

    def to_core(value):
        return lax.ppermute(value, "blk", [(i, i ^ 1) for i in range(2 * CHIPS)])

    def to_role(value):
        return lax.ppermute(value, "role", [(0, 1), (1, 0)])

    down = jnp.transpose(qkv_down, (0, 2, 1))
    def to_x(value):
        return lax.ppermute(value, "blk", [(i, i ^ 2) for i in range(2 * CHIPS)])

    def from_row(value, dy):
        pairs = [((i + 4 * dy) % (2 * CHIPS), i) for i in range(2 * CHIPS)]
        return lax.ppermute(value, "blk", pairs)

    place = jnp.reshape(blk, (1,))
    hid, core_hid, x_hid, cross_hid, weights = call(
        pack_body,
        [place, block_tenant],
        [prompt_hidden, qkv_up, jnp.transpose(out_down, (0, 2, 1)), out_up],
        [pl.BlockSpec(memory_space=pltpu.HBM)] * 4,
        [shape((BLOCK + ROWS, 4 * CHUNK))] * 4 + [shape((7, RANK, CHUNK))],
        [
            pltpu.VMEM(prompt_hidden.shape, BF16),
            pltpu.VMEM(qkv_up.shape, BF16),
            pltpu.VMEM((7, RANK, CHUNK), BF16),
            pltpu.VMEM((ROWS, 4 * CHUNK), BF16),
            pltpu.SemaphoreType.DMA((25,)),
        ],
        63,
        out_specs=[pl.BlockSpec(memory_space=pl.ANY)] * 5,
    )
    weights = lax.all_gather(weights, "blk")
    cross_hid = lax.ppermute(cross_hid, "blk", [(i, i ^ 3) for i in range(2 * CHIPS)])
    x_hid, core_hid = to_x(x_hid), to_core(core_hid)
    downs = [down, from_row(down, 1), from_row(down, 3), from_row(down, 2)]
    base, base_send = call(
        base_body,
        [lax.optimization_barrier((ids, x_hid))[0]],
        [prompt_qkv, row_cache],
        [pl.BlockSpec(memory_space=pltpu.HBM)] * 2,
        [shape((BLOCK, PACKED))] * 2,
        [pltpu.SemaphoreType.DMA((2 * (3 + 2 * (LIVE - 1)),))],
        out_specs=[pl.BlockSpec(memory_space=pl.ANY)] * 2,
    )
    base_oth = to_core(base_send)
    oth = to_core(block_tenant)
    row_hid = jnp.pad(row_hidden, ((0, ROWS - LIVE), (0, 0)))
    row_base = jnp.pad(row_qkv, ((0, ROWS - LIVE), (0, 0)))

    part, part_x = call(
        low_body,
        [ids],
        [hid, core_hid, x_hid, cross_hid, row_hid, *downs],
        [None] * 9,
        [shape((LOW_ROWS, HEAD))] * 2,
    )
    mine = (part.astype(F32) + to_x(part_x).astype(F32)).astype(BF16)
    mine = (mine.astype(F32) + to_core(mine).astype(F32)).astype(BF16)
    theirs = to_role(mine)
    row_columns = [
        spec((ROWS, HEADS * HEAD), lambda s: (0, s[HEAD_ID])),
        spec((ROWS, HEAD), lambda s: (0, 32 + s[HEAD_ID])),
        spec((ROWS, HEAD), lambda s: (0, 36 + s[HEAD_ID])),
    ]
    q, kv = call(
        proj_body,
        [ids, oth],
        [mine, theirs, base, base_oth] + [row_base] * 3 + [weights] * 3,
        [None] * 4
        + row_columns
        + [spec((2 * CHIPS, 1, RANK, CHUNK), lambda s, i=i: (0, i, 0, 0)) for i in range(3)],
        [shape((2 * BLOCK, HEADS * HEAD)), shape((2 * BLOCK + HEADS * LIVE, 2 * HEAD))],
        [pltpu.VMEM((CHIPS, 2, RANK, 5 * HEAD), BF16)],
        48,
    )
    kvs = gather_chips(kv)
    ctx, row_ctx = call(
        attend_body,
        [ids],
        [q, *kvs],
        [None] * (1 + CHIPS),
        [shape((2 * BLOCK, HEADS * HEAD)), shape((ROWS, HEADS * HEAD), F32)],
        [pltpu.VMEM((CHIPS * 2 * BLOCK, HEAD), BF16), pltpu.VMEM((CHIPS * 2 * BLOCK, 2 * HEAD), BF16)],
        32,
    )
    own, other = call(
        factor_body,
        [ids, oth],
        [ctx, row_ctx, weights, weights],
        [None, None]
        + [spec((4, 1, RANK, CHUNK), lambda s, t=t: (s[HEAD_ID], 3 + t, 0, 0)) for t in range(2)],
        [shape((RANK + ROWS, BLOCK)), shape((RANK + ROWS, BLOCK))],
        limit=48,
    )
    mine = (own.astype(F32) + to_core(other).astype(F32)).astype(BF16)
    return tuple(
        call(
            out_body,
            [ids],
            [mine, to_role(mine), weights, out_up],
            [None, None, spec((2 * CHIPS, 1, RANK, CHUNK), lambda s: (0, 5 + s[OWN], 0, 0)), None],
            [shape(prompt_hidden.shape), shape((LIVE, CHUNK))],
            limit=48,
        )
    )


def solution(mesh):
    in_specs = (
        P(("grp", "blk"), "role"),
        P(("grp", "blk"), None),
        P(("grp", "blk")),
        P("grp", None),
        P("grp", None),
        P("grp"),
        P("grp", "blk", None),
        P("grp"),
        P(None, ("role", "blk"), None),
        P(None, None, "blk"),
        P(None, "blk", None),
        P(None, None, ("role", "blk")),
    )
    out_specs = (P(("grp", "blk"), "role"), P("grp", ("role", "blk")))
    return jax.shard_map(
        per_device, mesh=mesh, in_specs=in_specs, out_specs=out_specs, check_vma=False
    )
```
